32 devices in a mesh: wide: 8 (over z, x), narrow: 4 (over y, core).
Axes of the slice: x: 2, y: 2, z: 4, core: 2. Of those that a mesh axis runs over, the one named last changes fastest.
Arguments:
- hidden_in: bfloat16 [512, 2048], P(('wide', 'narrow')), may hold values from -6 to 6
- queries: bfloat16 [512, 2048], P(('wide', 'narrow')), may hold values from -6 to 6
- cache_key: bfloat16 [512, 128, 256], P(('wide', 'narrow')), may hold values from -6 to 6
- cache_value: bfloat16 [512, 128, 256], P(('wide', 'narrow')), may hold values from -6 to 6
- new_key: bfloat16 [512, 256], P(('wide', 'narrow')), may hold values from -6 to 6
- new_value: bfloat16 [512, 256], P(('wide', 'narrow')), may hold values from -6 to 6
- lengths: int32 [512], P(('wide', 'narrow')), may hold values from 2 to 128, as said below
- norm_gain: bfloat16 [2048], replicated, may hold values from 0.5 to 1.5
- gate_codes: bfloat16 [32, 2048, 384], P(('wide', 'narrow')), may hold values from -4 to 4
- gate_scale: float32 [32, 16, 3], P(('wide', 'narrow')), may hold values from 0.011048543 to 0.044194173
- up_codes: bfloat16 [32, 2048, 384], P(('wide', 'narrow')), may hold values from -4 to 4
- up_scale: float32 [32, 16, 3], P(('wide', 'narrow')), may hold values from 0.011048543 to 0.044194173
- down_codes: bfloat16 [32, 384, 2048], P(('wide', 'narrow')), may hold values from -4 to 4
- down_scale: float32 [32, 3, 16], P(('wide', 'narrow')), may hold values from 0.018042196 to 0.07216878
- think_ids: int32 [512, 8], P(('wide', 'narrow')), may hold values from 0 to 15, all different within a row; in each aligned block of 16 rows (0 to 15, 16 to 31, ...) at most 16 rows name the same one
- think_gates: float32 [512, 8], P(('wide', 'narrow')), may hold values from 0.05 to 0.3
- talker_source: int32 [512], P(('wide', 'narrow')), may hold values from 0 to 511, as said below
- talker_gain: bfloat16 [2048], replicated, may hold values from 0.5 to 1.5
- talk_gate_w: bfloat16 [4, 2048, 384], P('narrow'), may hold values from -0.125 to 0.125
- talk_up_w: bfloat16 [4, 2048, 384], P('narrow'), may hold values from -0.125 to 0.125
- talk_down_w: bfloat16 [4, 384, 1024], P('narrow'), may hold values from -0.3125 to 0.3125
- talk_ids: int32 [512, 2], P(('wide', 'narrow')), may hold values from 0 to 3, all different within a row; in each aligned block of 16 rows (0 to 15, 16 to 31, ...) at most 16 rows name the same one
- talk_gates: float32 [512, 2], P(('wide', 'narrow')), may hold values from 0.3 to 0.7
Outputs:
- thinker_out: bfloat16 [512, 2048], P(('wide', 'narrow'))
- talker_out: bfloat16 [512, 1024], P(('wide', 'narrow'))
The draws below stay inside these ranges and needn't reach their ends.
Inputs may be any that keep to these rules, and one draw needn't show every extreme that they name: `think_ids`: each row names 8 different thinker experts; among the rows of one device no expert is named by more than 16 rows. `talk_ids`: each position names 2 different talker experts; among the positions of one device no expert is named by more than 16. `lengths`: some row uses all 128 cached positions. `talker_source`: A permutation of the rows. The row feeding a talker position lies on the same narrow index as the position. The rows of one device feed positions on exactly 8 devices, 2 positions on each.
All inputs are finite; a program needn't handle non-finite values.
Results may differ from the reference program's by a relative error of at most 0.018.
Values may be sent and summed in bfloat16 or wider, within the bound.
A program may use at most 64 MiB of HBM per device.

```python
import math
import jax
import jax.numpy as jnp
import numpy as np
from jax import lax

D = 2048
HEADS = 16
KV_HEADS = 2
HEAD_DIM = 128
CTX = 128
ROWS_DEV = 16
FH = 384
BLK = 128
TOP = 8
THINK_EXP = 16
CAP = 16
TD = 1024
TF = 384
TALK_EXP = 4
TTOP = 2
TCAP = 16
RCAP = 2
ROWS = 512
N_WIDE = 8
N_NARROW = 4


def draw_lengths(key, part):
    length_key, row_key = jax.random.split(key)
    drawn = jax.random.randint(length_key, (ROWS,), 2, CTX + 1)
    longest = jax.random.randint(row_key, (), 0, ROWS)
    return jnp.where(jnp.arange(ROWS) == longest, CTX, drawn).astype(jnp.int32)


def draw_talker_source(key, part):
    half_away = N_WIDE // 2
    before = N_WIDE - 1
    remaining = jnp.array([value for value in range(N_WIDE) if value != half_away and value != before], dtype=jnp.int32)
    columns = []
    for column in range(N_NARROW):
        shift_key, slot_key = jax.random.split(jax.random.fold_in(key, column))
        mixed = remaining[jax.random.permutation(shift_key, N_WIDE - 2)]
        leading = jnp.array([half_away, before], dtype=jnp.int32)
        shifts = jnp.concatenate([leading, mixed])[:ROWS_DEV // RCAP]
        slots = jax.random.permutation(slot_key, ROWS_DEV)
        offsets = shifts[jnp.arange(ROWS_DEV) // RCAP]
        target = jnp.arange(N_WIDE)[:, None]
        source_wide = (target + offsets[None, :]) % N_WIDE
        columns.append((source_wide * N_NARROW + column) * ROWS_DEV + slots[None, :])
    stacked = jnp.stack(columns, axis=1)
    return stacked.reshape(ROWS).astype(jnp.int32)


def background_draw(key, block_shape):
    return jax.random.truncated_normal(key, -6.0, 6.0, block_shape, jnp.float32)


def planted_heads(key):
    base_key = jax.random.fold_in(key, 9001)
    sign_key, slot_key, head_key = jax.random.split(base_key, 3)
    device_count = ROWS // ROWS_DEV
    sign_pattern = jnp.where(jax.random.bernoulli(sign_key, 0.5, (ROWS, HEAD_DIM)), 1.0, -1.0).astype(jnp.float32)
    chosen_slot = jax.random.randint(slot_key, (device_count,), 0, ROWS_DEV)
    chosen_head = jax.random.randint(head_key, (device_count,), 0, HEADS)
    row_index = jnp.arange(ROWS)
    row_owner = row_index // ROWS_DEV
    marked = row_index % ROWS_DEV == chosen_slot[row_owner]
    strength = 4.0 + (row_owner % 3).astype(jnp.float32)
    return (marked, strength, chosen_head[row_owner], sign_pattern)


def draw_queries(key, part):
    marked, strength, head_of, sign_pattern = planted_heads(key)
    background = background_draw(jax.random.fold_in(key, 11), (ROWS, HEADS, HEAD_DIM))
    aimed = marked[:, None] & (jnp.arange(HEADS)[None, :] == head_of[:, None])
    planted = strength[:, None, None] * sign_pattern[:, None, :]
    filled = jnp.where(aimed[:, :, None], planted, background)
    return filled.reshape(ROWS, HEADS * HEAD_DIM).astype(jnp.bfloat16)


def draw_cache_key(key, part):
    marked, strength, head_of, sign_pattern = planted_heads(key)
    background = background_draw(jax.random.fold_in(key, 12), (ROWS, CTX, KV_HEADS, HEAD_DIM))
    key_group = head_of // (HEADS // KV_HEADS)
    nearer = strength - 2.0 / (strength * HEAD_DIM ** 0.5)
    places = jnp.arange(CTX)
    level = jnp.where(places[None, :] == 0, strength[:, None], nearer[:, None])
    in_group = jnp.arange(KV_HEADS)[None, :] == key_group[:, None]
    aimed = marked[:, None, None] & (places < 2)[None, :, None] & in_group[:, None, :]
    planted = level[:, :, None, None] * sign_pattern[:, None, None, :]
    filled = jnp.where(aimed[:, :, :, None], planted, background)
    return filled.reshape(ROWS, CTX, KV_HEADS * HEAD_DIM).astype(jnp.bfloat16)


def level_of(key, extent, pieces, smallest, top_value):
    loudness, own = 1.0, jax.random.fold_in(key, 6)
    for axis_at, blocks in pieces:
        steps = jnp.exp(jax.random.uniform(jax.random.fold_in(own, axis_at), (blocks,), jnp.float32, smallest / len(pieces), top_value / len(pieces)))
        loudness = loudness * jnp.repeat(steps, extent[axis_at] // blocks).reshape([-1 if axis == axis_at else 1 for axis in range(len(extent))])
    return loudness


def routed_block(stream_key, own, number, rows, count, top, most, lean):
    order = jax.random.permutation(stream_key, count)
    crowded, common = portions_of(count, rows * top, most, lean, True), portions_of(count, rows * top, most, lean, False)
    places = jnp.arange(count)

    def named(tallies, offset_by):
        used = int((tallies > 0).sum())
        fixed = max(1, used // 4)
        shifted = fixed + (places - fixed + offset_by * (used - fixed)) % max(1, count - fixed)
        return jnp.zeros((count,), jnp.int32).at[order[jnp.where(places < fixed, places, shifted)]].set(jnp.asarray(tallies, jnp.int32))

    tallies = jnp.where(number % 4 == 0, named(crowded, number // 4), named(common, number - number // 4 - 1))
    mixed = jax.random.permutation(jax.random.fold_in(own, 3), count)
    giver, sink = mixed[0:count // 2 * 2:2], mixed[1:count // 2 * 2:2]
    room = jnp.minimum(tallies[giver] - 1, most - tallies[sink]) // 2
    room = jnp.where((giver == order[0]) | (sink == order[0]) | (tallies[sink] == 0), 0, jnp.maximum(room, 0))
    shifted = jax.random.randint(jax.random.fold_in(own, 4), (count // 2,), 0, 1 << 20) % (room + 1)
    tallies = tallies.at[giver].add(-shifted).at[sink].add(shifted)
    members = jnp.searchsorted(jnp.cumsum(tallies), jnp.arange(rows * top), side="right").astype(jnp.int32)
    grid = members.reshape(top, rows).T
    grid = grid[jax.random.permutation(jax.random.fold_in(own, 1), rows)]
    offset_by = jax.random.randint(jax.random.fold_in(own, 2), (rows, 1), 0, top)
    return jnp.take_along_axis(grid, (jnp.arange(top)[None, :] + offset_by) % top, axis=1)


def portions_of(count, total, reach, lean, full):
    loads = [(1 << 20) // math.isqrt(grade ** lean) + 1 for grade in range(1, count + 1)]
    largest = reach if full else min(reach, max(-(-total // count), total * loads[0] // sum(loads)))
    least = 1 if total - largest >= count - 1 else 0
    counts, spare = [largest] + [least] * (count - 1), total - largest - least * (count - 1)
    while spare > 0:
        candidates = [i for i in range(1, count) if counts[i] < largest] or [i for i in range(1, count) if counts[i] < reach]
        pool, left = sum([loads[i] for i in candidates]), spare
        for i in candidates:
            addition = min(reach - counts[i], max(1, left * loads[i] // pool), spare)
            counts[i] = counts[i] + addition
            spare = spare - addition
    return np.array(counts)


def centred(stream_key, shape, scale, bound, shards=(), held_as=jnp.bfloat16):
    entries = scale * jax.random.normal(stream_key, shape, jnp.float32)
    if shards:
        entries = entries * level_of(stream_key, shape, shards, -0.22, 0.18)
    return jnp.clip(entries, -bound, bound).astype(held_as)


def setup_inputs(seed: int = 0) -> dict:
    splits = jax.random.split(jax.random.key(seed), 24)
    hidden_in = centred(splits[0], (ROWS, D), 1.0, 6.0, ((0, 32),))
    queries = draw_queries(jax.random.fold_in(splits[23], 71), 0)
    cache_key = draw_cache_key(jax.random.fold_in(splits[23], 71), 0)
    cache_value = centred(splits[3], (ROWS, CTX, KV_HEADS * HEAD_DIM), 1.0, 6.0, ((0, 32),))
    new_key = centred(splits[4], (ROWS, KV_HEADS * HEAD_DIM), 1.0, 6.0, ((0, 32),))
    new_value = centred(splits[5], (ROWS, KV_HEADS * HEAD_DIM), 1.0, 6.0, ((0, 32),))
    lengths = draw_lengths(jax.random.fold_in(splits[23], 71), 0)
    norm_gain = jnp.clip(1.0 + 0.1 * jax.random.normal(splits[7], (D,), jnp.float32), 0.5, 1.5).astype(jnp.bfloat16)
    gate_codes = centred(splits[8], (2 * THINK_EXP, D, FH), 1.0, 4.0, ((0, 32),))
    gate_scale = jnp.clip(jnp.exp(math.log(0.044194173) - 1.3862944 * jax.random.uniform(splits[9], (2 * THINK_EXP, D // BLK, FH // BLK), jnp.float32) ** level_of(splits[9], (2 * THINK_EXP, D // BLK, FH // BLK), ((0, 32),), -0.2, 0.2)), 0.011048543, 0.044194173)
    up_codes = centred(splits[10], (2 * THINK_EXP, D, FH), 1.0, 4.0, ((0, 32),))
    up_scale = jnp.clip(jnp.exp(math.log(0.044194173) - 1.3862944 * jax.random.uniform(splits[11], (2 * THINK_EXP, D // BLK, FH // BLK), jnp.float32) ** level_of(splits[11], (2 * THINK_EXP, D // BLK, FH // BLK), ((0, 32),), -0.2, 0.2)), 0.011048543, 0.044194173)
    down_codes = centred(splits[12], (2 * THINK_EXP, FH, D), 1.0, 4.0, ((0, 32),))
    down_scale = jnp.clip(jnp.exp(math.log(0.07216878) - 1.3862944 * jax.random.uniform(splits[13], (2 * THINK_EXP, FH // BLK, D // BLK), jnp.float32) ** level_of(splits[13], (2 * THINK_EXP, FH // BLK, D // BLK), ((0, 32),), -0.2, 0.2)), 0.018042196, 0.07216878)
    think_ids_keys = jax.random.split(jax.random.fold_in(splits[14], 1), ROWS // ROWS_DEV)
    think_ids_turns = jax.random.permutation(jax.random.fold_in(splits[14], 3), ROWS // ROWS_DEV)
    think_ids = jax.vmap(lambda own, number: routed_block(jax.random.fold_in(splits[14], 2), own, number, ROWS_DEV, THINK_EXP, TOP, CAP, 2))(think_ids_keys, think_ids_turns).reshape((ROWS, TOP))
    think_gates = jnp.clip(0.05 + 0.25 * jax.random.uniform(splits[15], (ROWS, TOP), jnp.float32) ** level_of(splits[15], (ROWS, TOP), ((0, 32),), -0.2, 0.2), 0.05, 0.3)
    talker_source = draw_talker_source(jax.random.fold_in(splits[23], 71), 0)
    talker_gain = jnp.clip(1.0 + 0.1 * jax.random.normal(splits[17], (D,), jnp.float32), 0.5, 1.5).astype(jnp.bfloat16)
    talk_gate_w = centred(splits[18], (TALK_EXP, D, TF), D ** -0.5, 0.125, ((0, 4),))
    talk_up_w = centred(splits[19], (TALK_EXP, D, TF), D ** -0.5, 0.125, ((0, 4),))
    talk_down_w = centred(splits[20], (TALK_EXP, TF, TD), TF ** -0.5, 0.3125, ((0, 4),))
    talk_ids_keys = jax.random.split(jax.random.fold_in(splits[21], 1), ROWS // ROWS_DEV)
    talk_ids_turns = jax.random.permutation(jax.random.fold_in(splits[21], 3), ROWS // ROWS_DEV)
    talk_ids = jax.vmap(lambda own, number: routed_block(jax.random.fold_in(splits[21], 2), own, number, ROWS_DEV, TALK_EXP, TTOP, TCAP, 1))(talk_ids_keys, talk_ids_turns).reshape((ROWS, TTOP))
    talk_gates = jnp.clip(0.3 + 0.39999998 * jax.random.uniform(splits[22], (ROWS, TTOP), jnp.float32) ** level_of(splits[22], (ROWS, TTOP), ((0, 32),), -0.2, 0.2), 0.3, 0.7)
    return {"hidden_in": hidden_in, "queries": queries, "cache_key": cache_key, "cache_value": cache_value, "new_key": new_key, "new_value": new_value, "lengths": lengths, "norm_gain": norm_gain, "gate_codes": gate_codes, "gate_scale": gate_scale, "up_codes": up_codes, "up_scale": up_scale, "down_codes": down_codes, "down_scale": down_scale, "think_ids": think_ids, "think_gates": think_gates, "talker_source": talker_source, "talker_gain": talker_gain, "talk_gate_w": talk_gate_w, "talk_up_w": talk_up_w, "talk_down_w": talk_down_w, "talk_ids": talk_ids, "talk_gates": talk_gates}


EPSILON = 1e-06

def dequantize(code_block, scale_block):
    height, breadth = code_block.shape
    tiles = code_block.astype(jnp.float32).reshape(height // BLK, BLK, breadth // BLK, BLK)
    tiles = tiles * scale_block.astype(jnp.float32)[:, None, :, None]
    return tiles.reshape(height, breadth).astype(jnp.bfloat16)

def rms_norm(values, gain):
    values = values.astype(jnp.float32)
    spread = lax.optimization_barrier(jnp.mean(values * values, axis=-1, keepdims=True))
    return (values * lax.rsqrt(spread + EPSILON) * gain.astype(jnp.float32)).astype(jnp.bfloat16)

def swiglu(inputs, gate_dense, up_dense, down_dense):
    gated = jnp.dot(inputs, gate_dense, preferred_element_type=jnp.float32)
    lifted = jnp.dot(inputs, up_dense, preferred_element_type=jnp.float32)
    middle = (jax.nn.silu(gated) * lifted).astype(jnp.bfloat16)
    return jnp.dot(middle, down_dense, preferred_element_type=jnp.float32).astype(jnp.bfloat16)

def attend(queries, cache_key, cache_value, new_key, new_value, lengths):
    row_count = queries.shape[0]
    groups = HEADS // KV_HEADS
    scaling = HEAD_DIM ** (-0.5)
    asked = queries.astype(jnp.float32).reshape(row_count, KV_HEADS, groups, HEAD_DIM)
    cached_keys = cache_key.astype(jnp.float32).reshape(row_count, CTX, KV_HEADS, HEAD_DIM)
    cached_values = cache_value.astype(jnp.float32).reshape(row_count, CTX, KV_HEADS, HEAD_DIM)
    scores = jnp.einsum('rkgd,rtkd->rkgt', asked, cached_keys) * scaling
    fresh_score = jnp.einsum('rkgd,rkd->rkg', asked, new_key.astype(jnp.float32).reshape(row_count, KV_HEADS, HEAD_DIM)) * scaling
    places = jnp.arange(CTX, dtype=jnp.int32)
    live_mask = places[None, :] < lengths[:, None]
    scores = jnp.where(live_mask[:, None, None, :], scores, -jnp.inf)
    highest = jnp.maximum(lax.optimization_barrier(jnp.max(scores, axis=-1)), fresh_score)
    weights = jnp.exp(scores - highest[..., None])
    own_weight = jnp.exp(fresh_score - highest)
    totals = lax.optimization_barrier(jnp.sum(weights, axis=-1)) + own_weight
    probabilities = (weights / totals[..., None]).astype(jnp.bfloat16)
    own_prob = (own_weight / totals).astype(jnp.bfloat16)
    mixture = jnp.einsum('rkgt,rtkd->rkgd', probabilities.astype(jnp.float32), cached_values)
    newest = new_value.astype(jnp.float32).reshape(row_count, KV_HEADS, 1, HEAD_DIM)
    mixture = mixture + own_prob.astype(jnp.float32)[..., None] * newest
    return mixture.reshape(row_count, HEADS * HEAD_DIM)

def routed_sum(inputs, expert_ids, gate_weights, expert_count, limit, expert_fn, breadth):
    chosen = expert_ids[:, :, None] == jnp.arange(expert_count, dtype=jnp.int32)[None, None, :]
    picked = jnp.any(chosen, axis=1)
    weight_of = lax.optimization_barrier(jnp.sum(jnp.where(chosen, gate_weights.astype(jnp.float32)[:, :, None], jnp.float32(0.0)), axis=1))

    def add_expert(running, expert):
        column = picked[:, expert]
        indices = jnp.nonzero(column, size=limit, fill_value=0)[0].astype(jnp.int32)
        count = jnp.sum(column.astype(jnp.int32))
        valid = jnp.arange(limit, dtype=jnp.int32) < count
        scales = jnp.where(valid, weight_of[indices, expert], jnp.float32(0.0))
        result = expert_fn(expert, inputs[indices])
        return (running.at[indices].add(result * scales[:, None]), None)
    start = jnp.zeros((inputs.shape[0], breadth), jnp.float32)
    running, unused = lax.scan(add_expert, start, jnp.arange(expert_count, dtype=jnp.int32))
    return running

def reference(hidden_in, queries, cache_key, cache_value, new_key, new_value, lengths, norm_gain, gate_codes, gate_scale, up_codes, up_scale, down_codes, down_scale, think_ids, think_gates, talker_source, talker_gain, talk_gate_w, talk_up_w, talk_down_w, talk_ids, talk_gates):
    attended = attend(queries, cache_key, cache_value, new_key, new_value, lengths)
    residual = hidden_in.astype(jnp.float32) + attended
    normed = rms_norm(residual, norm_gain)

    def thinker_expert(expert, rows_in):
        output = jnp.zeros((rows_in.shape[0], D), jnp.float32)
        for half in range(2):
            index = 2 * expert + half
            gate_dense = dequantize(gate_codes[index], gate_scale[index])
            up_dense = dequantize(up_codes[index], up_scale[index])
            down_dense = dequantize(down_codes[index], down_scale[index])
            output = output + swiglu(rows_in, gate_dense, up_dense, down_dense).astype(jnp.float32)
        return output
    limit = min(ROWS, CAP * N_WIDE * N_NARROW)
    routed = routed_sum(normed, think_ids, think_gates, THINK_EXP, limit, thinker_expert, D)
    thinker_out = (residual + routed).astype(jnp.bfloat16)
    talker_in = thinker_out[talker_source]
    talker_normed = rms_norm(talker_in, talker_gain)

    def talker_expert(expert, rows_in):
        return swiglu(rows_in, talk_gate_w[expert], talk_up_w[expert], talk_down_w[expert]).astype(jnp.float32)
    talk_limit = min(ROWS, TCAP * N_WIDE * N_NARROW)
    talked = routed_sum(talker_normed, talk_ids, talk_gates, TALK_EXP, talk_limit, talker_expert, TD)
    return (thinker_out, talked.astype(jnp.bfloat16))
```

```python
import jax
import jax.numpy as jnp
from jax import lax
from jax.experimental import pallas as pl
from jax.experimental.pallas import tpu as pltpu
from jax.sharding import PartitionSpec as P

HEADS = 16
KV_HEADS = 2
HEAD_DIM = 128
BLK = 128
TOP = 8
TTOP = 2


EPSILON = 1e-06


def dequantize(code_block, scale_block):
    height, breadth = code_block.shape
    tiles = code_block.astype(jnp.float32).reshape(height // BLK, BLK, breadth // BLK, BLK)
    tiles = tiles * scale_block[:, None, :, None]
    return tiles.reshape(height, breadth).astype(jnp.bfloat16)


def rms_norm(values, gain):
    values = values.astype(jnp.float32)
    spread = jnp.mean(values * values, axis=-1, keepdims=True)
    return (values * lax.rsqrt(spread + EPSILON) * gain.astype(jnp.float32)).astype(jnp.bfloat16)


def swiglu(inputs, gate_dense, up_dense, down_dense):
    gated = jnp.dot(inputs, gate_dense, preferred_element_type=jnp.float32)
    lifted = jnp.dot(inputs, up_dense, preferred_element_type=jnp.float32)
    middle = (jax.nn.silu(gated) * lifted).astype(jnp.bfloat16)
    return jnp.dot(middle, down_dense, preferred_element_type=jnp.float32).astype(jnp.bfloat16)


def attend(queries, cache_key, cache_value, new_key, new_value, lengths):
    row_count = queries.shape[0]
    positions = cache_key.shape[1]
    groups = HEADS // KV_HEADS
    scaling = HEAD_DIM ** (-0.5)
    asked = queries.reshape(row_count, KV_HEADS, groups, HEAD_DIM)
    cached_keys = cache_key.reshape(row_count, positions, KV_HEADS, HEAD_DIM)
    cached_values = cache_value.reshape(row_count, positions, KV_HEADS, HEAD_DIM)
    scores = (
        jnp.einsum("rkgd,rtkd->rkgt", asked, cached_keys, preferred_element_type=jnp.float32)
        * scaling
    )
    newest_key = new_key.reshape(row_count, KV_HEADS, HEAD_DIM)
    fresh_score = (
        jnp.einsum("rkgd,rkd->rkg", asked, newest_key, preferred_element_type=jnp.float32) * scaling
    )
    places = jnp.arange(positions, dtype=jnp.int32)
    live_mask = places[None, :] < lengths[:, None]
    scores = jnp.where(live_mask[:, None, None, :], scores, -jnp.inf)
    highest = jnp.maximum(jnp.max(scores, axis=-1), fresh_score)
    weights = jnp.exp(scores - highest[..., None])
    own_weight = jnp.exp(fresh_score - highest)
    totals = jnp.sum(weights, axis=-1) + own_weight
    probabilities = (weights / totals[..., None]).astype(jnp.bfloat16)
    own_prob = (own_weight / totals).astype(jnp.bfloat16)
    mixture = jnp.einsum(
        "rkgt,rtkd->rkgd", probabilities, cached_values, preferred_element_type=jnp.float32
    )
    newest = new_value.reshape(row_count, KV_HEADS, 1, HEAD_DIM).astype(jnp.float32)
    mixture = mixture + own_prob.astype(jnp.float32)[..., None] * newest
    return mixture.reshape(row_count, HEADS * HEAD_DIM)


def slot_tables(expert_ids, gate_weights, expert_count, capacity):
    chosen = expert_ids[:, :, None] == jnp.arange(expert_count, dtype=jnp.int32)[None, None, :]
    picked = jnp.any(chosen, axis=1).astype(jnp.int32)
    weight_of = jnp.sum(jnp.where(chosen, gate_weights[:, :, None], jnp.float32(0.0)), axis=1)
    ranks = jnp.cumsum(picked, axis=0) - picked
    onehot = (picked[:, :, None] == 1) & (
        ranks[:, :, None] == jnp.arange(capacity, dtype=jnp.int32)[None, None, :]
    )
    placing = jnp.transpose(onehot, (1, 2, 0))
    return (placing, weight_of)


def local(
    hidden_in,
    queries,
    cache_key,
    cache_value,
    new_key,
    new_value,
    lengths,
    norm_gain,
    gate_codes,
    gate_scale,
    up_codes,
    up_scale,
    down_codes,
    down_scale,
    think_ids,
    think_gates,
    talker_source,
    talker_gain,
    talk_gate_w,
    talk_up_w,
    talk_down_w,
    talk_ids,
    talk_gates,
):
    wide_count = lax.axis_size("wide")
    narrow_count = lax.axis_size("narrow")
    row_count = hidden_in.shape[0]
    breadth = hidden_in.shape[1]
    attended = attend(queries, cache_key, cache_value, new_key, new_value, lengths)
    residual = hidden_in.astype(jnp.float32) + attended
    normed = rms_norm(residual, norm_gain)
    experts = wide_count * narrow_count // 2
    capacity = min(row_count, max(2, 2 * row_count * TOP // experts))
    placing, weight_of = slot_tables(think_ids, think_gates, experts, capacity)
    outgoing = jnp.einsum(
        "ecr,rd->ecd", placing.astype(jnp.bfloat16), normed, preferred_element_type=jnp.float32
    ).astype(jnp.bfloat16)
    doubled = jnp.broadcast_to(outgoing[:, None], (experts, 2, capacity, breadth)).reshape(
        wide_count, narrow_count, capacity, breadth
    )
    arrived = lax.all_to_all(
        lax.all_to_all(doubled, "wide", split_axis=0, concat_axis=0, tiled=True),
        "narrow",
        split_axis=1,
        concat_axis=1,
        tiled=True,
    )
    gate_dense = dequantize(gate_codes[0], gate_scale[0])
    up_dense = dequantize(up_codes[0], up_scale[0])
    down_dense = dequantize(down_codes[0], down_scale[0])
    produced = swiglu(arrived.reshape(-1, breadth), gate_dense, up_dense, down_dense)
    produced = produced.reshape(wide_count, narrow_count, capacity, breadth)
    returned = lax.all_to_all(
        lax.all_to_all(produced, "wide", split_axis=0, concat_axis=0, tiled=True),
        "narrow",
        split_axis=1,
        concat_axis=1,
        tiled=True,
    )
    paired = returned.reshape(experts, 2, capacity, breadth)
    summed = paired[:, 0].astype(jnp.float32) + paired[:, 1].astype(jnp.float32)
    combine = placing.astype(jnp.float32) * jnp.transpose(weight_of)[:, None, :]
    routed = jnp.einsum("ecr,ecd->rd", combine, summed, precision=lax.Precision.HIGHEST)
    thinker_out = (residual + routed).astype(jnp.bfloat16)
    own_wide = talker_source // row_count // narrow_count
    own_local = talker_source % row_count
    gathered = lax.all_gather(thinker_out, "wide", axis=0, tiled=True)
    talker_in = jnp.take(gathered, own_wide * row_count + own_local, axis=0)
    talker_normed = rms_norm(talker_in, talker_gain)
    talk_capacity = min(row_count, max(2, 2 * row_count * TTOP // narrow_count))
    talk_placing, talk_weight = slot_tables(talk_ids, talk_gates, narrow_count, talk_capacity)
    talk_outgoing = jnp.einsum(
        "ecr,rd->ecd",
        talk_placing.astype(jnp.bfloat16),
        talker_normed,
        preferred_element_type=jnp.float32,
    ).astype(jnp.bfloat16)
    incoming = lax.all_to_all(talk_outgoing, "narrow", split_axis=0, concat_axis=0, tiled=True)
    sources = incoming.shape[0]
    items = incoming.shape[1]
    result = swiglu(incoming.reshape(-1, breadth), talk_gate_w[0], talk_up_w[0], talk_down_w[0])
    talk_done = result.reshape(sources, items, -1)
    talk_back = lax.all_to_all(talk_done, "narrow", split_axis=0, concat_axis=0, tiled=True)
    talk_combine = talk_placing.astype(jnp.float32) * jnp.transpose(talk_weight)[:, None, :]
    talked = jnp.einsum(
        "ecr,ecd->rd", talk_combine, talk_back.astype(jnp.float32), precision=lax.Precision.HIGHEST
    )
    return (thinker_out, talked.astype(jnp.bfloat16))


EXT = 128
MESH = pl.DeviceIdType.MESH


def attention_kernel(
    hidden_ref, queries_ref, key_ref, value_ref, new_key_ref, new_value_ref, lengths_ref, gain_ref,
    ids_ref, gates_ref, residual_ref, extended_ref, asked, scores, mixture,
):
    rows = hidden_ref.shape[0]
    breadth = hidden_ref.shape[1]
    for head in range(HEADS):
        asked[:, head, :] = queries_ref[:, head * HEAD_DIM : (head + 1) * HEAD_DIM].astype(jnp.float32)
    scaling = HEAD_DIM ** (-0.5)
    lower = lax.broadcasted_iota(jnp.int32, (HEADS, HEAD_DIM), 0) < HEADS // KV_HEADS
    places = lax.broadcasted_iota(jnp.int32, (HEADS, HEAD_DIM), 1)
    contract = (((1,), (1,)), ((), ()))
    fresh = []
    for row in range(rows):
        query = asked[row]
        packed = query.astype(jnp.bfloat16)
        first = lax.dot_general(packed, key_ref[row, :, :HEAD_DIM], contract, preferred_element_type=jnp.float32)
        second = lax.dot_general(packed, key_ref[row, :, HEAD_DIM:], contract, preferred_element_type=jnp.float32)
        found = jnp.where(lower, first, second) * scaling
        scores[row] = jnp.where(places < lengths_ref[row], found, -jnp.inf)
        newest = jnp.where(
            lower,
            new_key_ref[row : row + 1, :HEAD_DIM].astype(jnp.float32),
            new_key_ref[row : row + 1, HEAD_DIM:].astype(jnp.float32),
        )
        fresh.append(jnp.sum(query * newest, axis=1, keepdims=True) * scaling)
    for row in range(rows):
        found = scores[row]
        highest = jnp.maximum(jnp.max(found, axis=1, keepdims=True), fresh[row])
        weights = jnp.exp(found - highest)
        own_weight = jnp.exp(fresh[row] - highest)
        totals = jnp.sum(weights, axis=1, keepdims=True) + own_weight
        probabilities = (weights / totals).astype(jnp.bfloat16)
        own_prob = (own_weight / totals).astype(jnp.bfloat16).astype(jnp.float32)
        first = jnp.dot(probabilities, value_ref[row, :, :HEAD_DIM], preferred_element_type=jnp.float32)
        second = jnp.dot(probabilities, value_ref[row, :, HEAD_DIM:], preferred_element_type=jnp.float32)
        newest = jnp.where(
            lower,
            new_value_ref[row : row + 1, :HEAD_DIM].astype(jnp.float32),
            new_value_ref[row : row + 1, HEAD_DIM:].astype(jnp.float32),
        )
        mixture[row] = jnp.where(lower, first, second) + own_prob * newest
    square = jnp.zeros((rows, HEAD_DIM), jnp.float32)
    for head in range(HEADS):
        columns = slice(head * HEAD_DIM, (head + 1) * HEAD_DIM)
        part = hidden_ref[:, columns].astype(jnp.float32) + mixture[:, head, :]
        residual_ref[:, columns] = part
        square = square + part * part
    spread = jnp.sum(square, axis=1, keepdims=True) / breadth
    factor = lax.rsqrt(spread + EPSILON)
    extended_ref[:, :breadth] = (residual_ref[...] * factor * gain_ref[...].astype(jnp.float32)).astype(jnp.bfloat16)
    lanes = lax.broadcasted_iota(jnp.int32, (rows, EXT), 1)
    named = lanes % 16
    weight = jnp.zeros((rows, EXT), jnp.float32)
    for choice in range(TOP):
        weight = weight + jnp.where(ids_ref[:, choice : choice + 1] == named, gates_ref[:, choice : choice + 1], 0.0)
    high = weight.astype(jnp.bfloat16).astype(jnp.float32)
    extended_ref[:, breadth:] = jnp.where(lanes < 16, high, weight - high).astype(jnp.bfloat16)


def expert_kernel(
    residual_ref, extended_ref, gate_scale_ref, up_scale_ref, down_scale_ref, meta_ref, place_ref, talker_gain_ref,
    gate_hbm, up_hbm, down_hbm, talk_gate_hbm, talk_up_hbm, talk_down_hbm,
    thinker_ref, talker_ref,
    gate_w, up_w, down_w, talk_gate_w, talk_up_w, talk_down_w, load_sem,
    rows_a, rows_b, kept, core_out, core_in, y_out, y_in, x_out, x_in, x_late_out, x_late_in, y_late_out, y_late_in,
    z_out, z_in, meta_in, meta_rows, talk_rows, spaced, talk_out, talk_in, send_sem, recv_sem,
):
    f32, bf16 = jnp.float32, jnp.bfloat16
    wide, narrow = lax.axis_index("wide"), lax.axis_index("narrow")
    z, x, y, c = wide // 2, wide % 2, narrow // 2, narrow % 2
    half = 1024

    def peer(dz, bx, by, bc):
        there = (z + dz) % 4 if dz else z
        return (there * 2 + (1 - x if bx else x), (1 - y if by else y) * 2 + (1 - c if bc else c))

    loads = []
    for number, (source, target) in enumerate((
        (gate_hbm, gate_w), (up_hbm, up_w), (down_hbm, down_w),
        (talk_gate_hbm, talk_gate_w), (talk_up_hbm, talk_up_w), (talk_down_hbm, talk_down_w),
    )):
        load = pltpu.make_async_copy(source.at[0], target, load_sem.at[number])
        load.start()
        loads.append(load)
    barrier = pltpu.get_barrier_semaphore()
    everyone = [
        (dz, bx, by, bc) for dz in range(4) for bx in range(2) for by in range(2) for bc in range(2) if dz or bx or by or bc
    ]
    for one in everyone:
        pl.semaphore_signal(barrier, inc=1, device_id=peer(*one), device_id_type=MESH)
    rows_a[0, 0, :, :half] = extended_ref[:, :half]
    rows_a[0, 0, :, half:] = extended_ref[:, 2 * half :]
    rows_b[0, 0] = extended_ref[:, half : 2 * half]
    meta_in[0] = meta_ref[0]
    pl.semaphore_wait(barrier, len(everyone))

    pending = []

    def send(source, target, to):
        number = len(pending)
        copy = pltpu.make_async_remote_copy(
            src_ref=source, dst_ref=target, send_sem=send_sem.at[number], recv_sem=recv_sem.at[number],
            device_id=peer(*to), device_id_type=MESH,
        )
        copy.start()
        pending.append(copy)
        return copy

    to_x, to_y, to_c = (0, 1, 0, 0), (0, 0, 1, 0), (0, 0, 0, 1)
    a_x = [send(rows_a.at[0, 0], rows_a.at[1, 0], to_x)]
    b_y = [send(rows_b.at[0, 0], rows_b.at[2, 0], to_y)]
    a_z, b_z = {}, {}
    for step in (2, 1, 3):
        a_z[step] = send(rows_a.at[0, 0], rows_a.at[0, 4 - step], (step, 0, 0, 0))
        b_z[step] = send(rows_b.at[0, 0], rows_b.at[0, 4 - step], (step, 0, 0, 0))
    a_y = [send(rows_a.at[0, 0], rows_a.at[2, 0], to_y)]
    b_x = [send(rows_b.at[0, 0], rows_b.at[1, 0], to_x)]
    meta_copies = []
    for dz in range(4):
        for bx in range(2):
            if dz or bx:
                meta_copies.append(
                    send(meta_ref.at[dz * 2 + bx], meta_in.at[(4 - dz) % 4 * 2 + bx], (dz, bx, 0, 0))
                )

    def scaled(weights, scales, row_block, column_blocks):
        rows = pl.ds(pl.multiple_of(row_block * BLK, BLK), BLK)
        for column in range(column_blocks):
            columns = slice(column * BLK, (column + 1) * BLK)
            weights[rows, columns] = (weights[rows, columns].astype(f32) * scales[0, row_block, column]).astype(bf16)

    loads[0].wait()
    loads[1].wait()

    def scale_inner(first, last):
        def body(row_block, carry):
            scaled(gate_w, gate_scale_ref, row_block, 3)
            scaled(up_w, up_scale_ref, row_block, 3)
            return carry

        lax.fori_loop(first, last, body, 0)

    scale_inner(0, 4)
    for step in (1, 3, 2):
        rel = 4 - step
        a_z[step].wait_recv()
        a_x.append(send(rows_a.at[0, rel], rows_a.at[1, rel], to_x))
        b_z[step].wait_recv()
        b_y.append(send(rows_b.at[0, rel], rows_b.at[2, rel], to_y))
        a_y.append(send(rows_a.at[0, rel], rows_a.at[2, rel], to_y))
        b_x.append(send(rows_b.at[0, rel], rows_b.at[1, rel], to_x))
    across = [send(rows_a.at[0], rows_a.at[4], to_c), send(rows_b.at[0], rows_b.at[4], to_c)]
    a_far, b_far = [], []
    for number, rel in enumerate((0, 3, 1, 2)):
        a_x[number].wait_recv()
        a_far.append(send(rows_a.at[1, rel], rows_a.at[3, rel], to_y))
        b_y[number].wait_recv()
        b_far.append(send(rows_b.at[2, rel], rows_b.at[3, rel], to_x))
        if number < 3:
            scale_inner(4 + number * 4, 8 + number * 4)
    across += [send(rows_a.at[1], rows_a.at[5], to_c), send(rows_b.at[2], rows_b.at[6], to_c)]
    loads[2].wait()

    def scale_outer(row_block, carry):
        scaled(down_w, down_scale_ref, row_block, 16)
        return carry

    lax.fori_loop(0, 3, scale_outer, 0)
    for copy in a_y + b_x:
        copy.wait_recv()
    across += [send(rows_a.at[2], rows_a.at[6], to_c), send(rows_b.at[1], rows_b.at[5], to_c)]
    for copy in a_far + b_far:
        copy.wait_recv()
    across += [send(rows_a.at[3], rows_a.at[7], to_c), send(rows_b.at[3], rows_b.at[7], to_c)]

    def weight_column(extras, first, second):
        lanes = lax.broadcasted_iota(jnp.int32, extras.shape, 1)
        return jnp.sum(jnp.where((lanes == first) | (lanes == second), extras.astype(f32), 0.0), axis=1, keepdims=True)

    expert = wide * 2 + narrow // 2

    def hidden_units(base, count):
        left = rows_a[base : base + count].reshape(count * 64, half + EXT)
        right = rows_b[base : base + count].reshape(count * 64, half)
        weight = weight_column(left[:, half:], expert, expert + 16)
        left = left[:, :half]
        gated = jnp.dot(left, gate_w[:half], preferred_element_type=f32)
        gated = gated + jnp.dot(right, gate_w[half:], preferred_element_type=f32)
        lifted = jnp.dot(left, up_w[:half], preferred_element_type=f32)
        lifted = lifted + jnp.dot(right, up_w[half:], preferred_element_type=f32)
        return (jax.nn.silu(gated) * lifted).astype(bf16), weight

    for copy in across:
        copy.wait_recv()
    middle, weight = hidden_units(4, 4)
    for column in range(4):
        columns = slice(column * 512, (column + 1) * 512)
        part = jnp.dot(middle, down_w[:, columns], preferred_element_type=f32) * weight
        core_out[column] = part.astype(bf16)
    core_copies = [send(core_out.at[column], core_in.at[column], to_c) for column in range(4)]
    middle, weight = hidden_units(0, 4)
    for column in range(4):
        columns = slice(column * 512, (column + 1) * 512)
        kept[column] = jnp.dot(middle, down_w[:, columns], preferred_element_type=f32) * weight
    for column in range(4):
        core_copies[column].wait_recv()
        kept[column] = kept[column] + core_in[column].astype(f32)

    def piece(group, rel, column):
        start = group * 64 + rel * 16
        return kept[column, start : start + 16, :]

    order = (2, 1, 3, 0)
    first_y, first_x = {}, {}
    for rel in order:
        for at in range(2):
            for column in range(2):
                span = slice(column * 512, (column + 1) * 512)
                y_out[rel, at * 16 : (at + 1) * 16, span] = piece(2 + at, rel, column).astype(bf16)
                x_out[rel, at * 16 : (at + 1) * 16, span] = piece(1 + 2 * at, rel, 2 + column).astype(bf16)
        first_y[rel] = send(y_out.at[rel], y_in.at[rel], to_y)
        first_x[rel] = send(x_out.at[rel], x_in.at[rel], to_x)
    late_x, late_y = {}, {}
    for rel in order:
        first_y[rel].wait_recv()
        first_x[rel].wait_recv()
        for column in range(2):
            span = slice(column * 512, (column + 1) * 512)
            x_late_out[rel, :, span] = (piece(1, rel, column) + y_in[rel, 16:, span].astype(f32)).astype(bf16)
            y_late_out[rel, :, span] = (piece(2, rel, 2 + column) + x_in[rel, 16:, span].astype(f32)).astype(bf16)
        late_x[rel] = send(x_late_out.at[rel], x_late_in.at[rel], to_x)
        late_y[rel] = send(y_late_out.at[rel], y_late_in.at[rel], to_y)
    own_left = own_right = None
    z_copies = {}
    for rel in order:
        late_x[rel].wait_recv()
        late_y[rel].wait_recv()
        sums = []
        for column in range(4):
            span = slice(column % 2 * 512, (column % 2 + 1) * 512)
            early, late = (y_in, x_late_in) if column < 2 else (x_in, y_late_in)
            sums.append(piece(0, rel, column) + early[rel, :16, span].astype(f32) + late[rel, :, span].astype(f32))
        if rel:
            for column in range(4):
                z_out[rel, :, column * 512 : (column + 1) * 512] = sums[column].astype(bf16)
            z_copies[rel] = send(z_out.at[rel], z_in.at[4 - rel], (rel, 0, 0, 0))
    for rel in (1, 2, 3):
        z_copies[rel].wait_recv()
    for copy in meta_copies:
        copy.wait_recv()
    for load in loads[3:]:
        load.wait()
    square = jnp.zeros((16, 512), f32)
    finals = []
    for column in range(4):
        span = slice(column * 512, (column + 1) * 512)
        total = residual_ref[:, span] + sums[column]
        for rel in (1, 2, 3):
            total = total + z_in[rel, :, span].astype(f32)
        final = total.astype(bf16)
        thinker_ref[:, span] = final
        final = final.astype(f32)
        finals.append(final)
        square = square + final * final
    factor = lax.rsqrt(jnp.sum(square, axis=1, keepdims=True) / 2048 + EPSILON)
    for slot in range(8):
        meta_rows[2 * slot : 2 * slot + 2, :] = meta_in[slot, 0:2, :]
    meta = meta_rows[...]
    picks = (meta[:, 4:5].astype(jnp.int32) == lax.broadcasted_iota(jnp.int32, (16, 16), 1)).astype(f32).astype(bf16)
    for column in range(4):
        span = slice(column * 512, (column + 1) * 512)
        normed = (finals[column] * factor * talker_gain_ref[:, span].astype(f32)).astype(bf16)
        talk_rows[0, :, span] = jnp.dot(picks, normed, preferred_element_type=f32).astype(bf16)
    high = meta.astype(bf16).astype(f32)
    lanes = lax.broadcasted_iota(jnp.int32, meta.shape, 1)
    talk_rows[0, :, 2048:] = jnp.where(lanes < 8, high, meta - high).astype(bf16)
    gathers = [send(talk_rows.at[0], talk_rows.at[v], (0, 0, v // 2, v % 2)) for v in (3, 2, 1)]
    for copy in gathers:
        copy.wait_recv()
    inputs = talk_rows[...].reshape(64, 2048 + EXT)
    weight = weight_column(inputs[:, 2048:], narrow, narrow + 8)
    inputs = inputs[:, :2048]
    gated = jnp.dot(inputs, talk_gate_w[...], preferred_element_type=f32)
    lifted = jnp.dot(inputs, talk_up_w[...], preferred_element_type=f32)
    middle = (jax.nn.silu(gated) * lifted).astype(bf16)
    result = jnp.dot(middle, talk_down_w[...], preferred_element_type=f32) * weight
    for column in range(8):
        spaced[:, column, :] = result[:, column * 128 : (column + 1) * 128]
    talk_out[...] = spaced[...].reshape(512, 128).astype(bf16).reshape(4, 8, 16, 128)
    backs = []
    for dz in (2, 1, 3, 0):
        for bx in range(2):
            for v in range(4):
                if dz or bx or v:
                    backs.append(
                        send(
                            talk_out.at[v, dz * 2 + bx], talk_in.at[v, (4 - dz) % 4 * 2 + bx], (dz, bx, v // 2, v % 2)
                        )
                    )
    talk_in[0, 0] = talk_out[0, 0]
    for copy in backs:
        copy.wait_recv()
    total = talk_in[0].astype(f32)
    for v in range(1, 4):
        total = total + talk_in[v].astype(f32)
    spaced[:16] = total.reshape(16, 8, 128)
    for column in range(8):
        part = spaced[:16, column, :].astype(bf16)
        talker_ref[:, column * 128 : (column + 1) * 128] = jnp.dot(
            place_ref[...], part, preferred_element_type=f32
        ).astype(bf16)
    for copy in pending:
        copy.wait_send()


def local_fused(
    hidden_in, queries, cache_key, cache_value, new_key, new_value, lengths, norm_gain, gate_codes, gate_scale,
    up_codes, up_scale, down_codes, down_scale, think_ids, think_gates, talker_source, talker_gain, talk_gate_w,
    talk_up_w, talk_down_w, talk_ids, talk_gates,
):
    f32, bf16 = jnp.float32, jnp.bfloat16
    vmem, smem, hbm = (pl.BlockSpec(memory_space=s) for s in (pltpu.VMEM, pltpu.SMEM, pl.ANY))
    rows, breadth = hidden_in.shape
    wide = lax.axis_index("wide")
    residual, extended = pl.pallas_call(
        attention_kernel,
        out_shape=(
            jax.ShapeDtypeStruct((rows, breadth), f32),
            jax.ShapeDtypeStruct((rows, breadth + EXT), bf16),
        ),
        in_specs=[vmem] * 6 + [smem] + [vmem] * 3,
        out_specs=(vmem, vmem),
        scratch_shapes=[pltpu.VMEM((rows, HEADS, HEAD_DIM), f32)] * 3,
        compiler_params=pltpu.CompilerParams(vmem_limit_bytes=24 * 2**20),
    )(
        hidden_in, queries, cache_key, cache_value, new_key, new_value, lengths, norm_gain[None, :], think_ids,
        think_gates,
    )
    source_wide = talker_source // (rows * 4)
    relative = (source_wide // 2 - wide // 2) % 4 * 2 + (source_wide % 2 + wide % 2) % 2
    same = (relative[:, None] == relative[None, :]) & (jnp.arange(rows)[None, :] < jnp.arange(rows)[:, None])
    slot = relative * 2 + jnp.sum(same.astype(jnp.int32), axis=1)
    place = slot[:, None] == jnp.arange(rows)[None, :]
    weights = jnp.sum(
        jnp.where(talk_ids[:, :, None] == jnp.arange(4)[None, None, :], talk_gates[:, :, None], 0.0),
        axis=1,
    )
    origin = (talker_source % rows).astype(f32)[:, None]
    nothing = jnp.zeros((rows, 3), f32)
    columns = jnp.concatenate([weights, origin, nothing, weights, jnp.zeros((rows, 116), f32)], axis=1)
    by_slot = jnp.sum(jnp.where(place[:, :, None], columns[:, None, :], 0.0), axis=0)
    meta = jnp.pad(by_slot.reshape(8, 2, EXT), ((0, 0), (0, 6), (0, 0)))
    return pl.pallas_call(
        expert_kernel,
        out_shape=(jax.ShapeDtypeStruct((rows, breadth), bf16), jax.ShapeDtypeStruct((rows, 1024), bf16)),
        in_specs=[vmem, vmem, smem, smem, smem, vmem, vmem, vmem] + [hbm] * 6,
        out_specs=(vmem, vmem),
        scratch_shapes=[
            pltpu.VMEM((2048, 384), bf16),
            pltpu.VMEM((2048, 384), bf16),
            pltpu.VMEM((384, 2048), bf16),
            pltpu.VMEM((2048, 384), bf16),
            pltpu.VMEM((2048, 384), bf16),
            pltpu.VMEM((384, 1024), bf16),
            pltpu.SemaphoreType.DMA((6,)),
            pltpu.VMEM((8, 4, 16, 1024 + EXT), bf16),
            pltpu.VMEM((8, 4, 16, 1024), bf16),
            pltpu.VMEM((4, 256, 512), f32),
            pltpu.VMEM((4, 256, 512), bf16),
            pltpu.VMEM((4, 256, 512), bf16),
            pltpu.VMEM((4, 32, 1024), bf16),
            pltpu.VMEM((4, 32, 1024), bf16),
            pltpu.VMEM((4, 32, 1024), bf16),
            pltpu.VMEM((4, 32, 1024), bf16),
            pltpu.VMEM((4, 16, 1024), bf16),
            pltpu.VMEM((4, 16, 1024), bf16),
            pltpu.VMEM((4, 16, 1024), bf16),
            pltpu.VMEM((4, 16, 1024), bf16),
            pltpu.VMEM((4, 16, 2048), bf16),
            pltpu.VMEM((4, 16, 2048), bf16),
            pltpu.VMEM((8, 8, EXT), f32),
            pltpu.VMEM((16, EXT), f32),
            pltpu.VMEM((4, 16, 2048 + EXT), bf16),
            pltpu.VMEM((64, 8, 128), f32),
            pltpu.VMEM((4, 8, 16, 128), bf16),
            pltpu.VMEM((4, 8, 16, 128), bf16),
            pltpu.SemaphoreType.DMA((112,)),
            pltpu.SemaphoreType.DMA((112,)),
        ],
        compiler_params=pltpu.CompilerParams(
            collective_id=0, has_side_effects=True, vmem_limit_bytes=44 * 2**20
        ),
    )(
        residual, extended, gate_scale, up_scale, down_scale, meta, place.astype(bf16), talker_gain[None, :],
        gate_codes, up_codes, down_codes, talk_gate_w, talk_up_w, talk_down_w,
    )


def solution(mesh):
    return jax.shard_map(
        local_fused if mesh.shape["wide"] == 8 and mesh.shape["narrow"] == 4 else local,
        mesh=mesh,
        in_specs=(
            P(("wide", "narrow"), None),
            P(("wide", "narrow"), None),
            P(("wide", "narrow"), None, None),
            P(("wide", "narrow"), None, None),
            P(("wide", "narrow"), None),
            P(("wide", "narrow"), None),
            P(("wide", "narrow")),
            P(),
            P(("wide", "narrow"), None, None),
            P(("wide", "narrow"), None, None),
            P(("wide", "narrow"), None, None),
            P(("wide", "narrow"), None, None),
            P(("wide", "narrow"), None, None),
            P(("wide", "narrow"), None, None),
            P(("wide", "narrow"), None),
            P(("wide", "narrow"), None),
            P(("wide", "narrow")),
            P(),
            P("narrow", None, None),
            P("narrow", None, None),
            P("narrow", None, None),
            P(("wide", "narrow"), None),
            P(("wide", "narrow"), None),
        ),
        out_specs=(P(("wide", "narrow"), None), P(("wide", "narrow"), None)),
        check_vma=False,
    )
```

```python
import jax
import jax.numpy as jnp
from jax import lax
from jax.experimental import pallas as pl
from jax.experimental.pallas import tpu as pltpu
from jax.sharding import PartitionSpec as P

HEADS = 16
KV_HEADS = 2
HEAD_DIM = 128
BLK = 128
TOP = 8
TTOP = 2


EPSILON = 1e-06


def dequantize(code_block, scale_block):
    height, breadth = code_block.shape
    tiles = code_block.astype(jnp.float32).reshape(height // BLK, BLK, breadth // BLK, BLK)
    tiles = tiles * scale_block[:, None, :, None]
    return tiles.reshape(height, breadth).astype(jnp.bfloat16)


def rms_norm(values, gain):
    values = values.astype(jnp.float32)
    spread = jnp.mean(values * values, axis=-1, keepdims=True)
    return (values * lax.rsqrt(spread + EPSILON) * gain.astype(jnp.float32)).astype(jnp.bfloat16)


def swiglu(inputs, gate_dense, up_dense, down_dense):
    gated = jnp.dot(inputs, gate_dense, preferred_element_type=jnp.float32)
    lifted = jnp.dot(inputs, up_dense, preferred_element_type=jnp.float32)
    middle = (jax.nn.silu(gated) * lifted).astype(jnp.bfloat16)
    return jnp.dot(middle, down_dense, preferred_element_type=jnp.float32).astype(jnp.bfloat16)


def attend(queries, cache_key, cache_value, new_key, new_value, lengths):
    row_count = queries.shape[0]
    positions = cache_key.shape[1]
    groups = HEADS // KV_HEADS
    scaling = HEAD_DIM ** (-0.5)
    asked = queries.reshape(row_count, KV_HEADS, groups, HEAD_DIM)
    cached_keys = cache_key.reshape(row_count, positions, KV_HEADS, HEAD_DIM)
    cached_values = cache_value.reshape(row_count, positions, KV_HEADS, HEAD_DIM)
    scores = (
        jnp.einsum("rkgd,rtkd->rkgt", asked, cached_keys, preferred_element_type=jnp.float32)
        * scaling
    )
    newest_key = new_key.reshape(row_count, KV_HEADS, HEAD_DIM)
    fresh_score = (
        jnp.einsum("rkgd,rkd->rkg", asked, newest_key, preferred_element_type=jnp.float32) * scaling
    )
    places = jnp.arange(positions, dtype=jnp.int32)
    live_mask = places[None, :] < lengths[:, None]
    scores = jnp.where(live_mask[:, None, None, :], scores, -jnp.inf)
    highest = jnp.maximum(jnp.max(scores, axis=-1), fresh_score)
    weights = jnp.exp(scores - highest[..., None])
    own_weight = jnp.exp(fresh_score - highest)
    totals = jnp.sum(weights, axis=-1) + own_weight
    probabilities = (weights / totals[..., None]).astype(jnp.bfloat16)
    own_prob = (own_weight / totals).astype(jnp.bfloat16)
    mixture = jnp.einsum(
        "rkgt,rtkd->rkgd", probabilities, cached_values, preferred_element_type=jnp.float32
    )
    newest = new_value.reshape(row_count, KV_HEADS, 1, HEAD_DIM).astype(jnp.float32)
    mixture = mixture + own_prob.astype(jnp.float32)[..., None] * newest
    return mixture.reshape(row_count, HEADS * HEAD_DIM)


def slot_tables(expert_ids, gate_weights, expert_count, capacity):
    chosen = expert_ids[:, :, None] == jnp.arange(expert_count, dtype=jnp.int32)[None, None, :]
    picked = jnp.any(chosen, axis=1).astype(jnp.int32)
    weight_of = jnp.sum(jnp.where(chosen, gate_weights[:, :, None], jnp.float32(0.0)), axis=1)
    ranks = jnp.cumsum(picked, axis=0) - picked
    onehot = (picked[:, :, None] == 1) & (
        ranks[:, :, None] == jnp.arange(capacity, dtype=jnp.int32)[None, None, :]
    )
    placing = jnp.transpose(onehot, (1, 2, 0))
    return (placing, weight_of)


def local(
    hidden_in,
    queries,
    cache_key,
    cache_value,
    new_key,
    new_value,
    lengths,
    norm_gain,
    gate_codes,
    gate_scale,
    up_codes,
    up_scale,
    down_codes,
    down_scale,
    think_ids,
    think_gates,
    talker_source,
    talker_gain,
    talk_gate_w,
    talk_up_w,
    talk_down_w,
    talk_ids,
    talk_gates,
):
    wide_count = lax.axis_size("wide")
    narrow_count = lax.axis_size("narrow")
    row_count = hidden_in.shape[0]
    breadth = hidden_in.shape[1]
    attended = attend(queries, cache_key, cache_value, new_key, new_value, lengths)
    residual = hidden_in.astype(jnp.float32) + attended
    normed = rms_norm(residual, norm_gain)
    experts = wide_count * narrow_count // 2
    capacity = min(row_count, max(2, 2 * row_count * TOP // experts))
    placing, weight_of = slot_tables(think_ids, think_gates, experts, capacity)
    outgoing = jnp.einsum(
        "ecr,rd->ecd", placing.astype(jnp.bfloat16), normed, preferred_element_type=jnp.float32
    ).astype(jnp.bfloat16)
    doubled = jnp.broadcast_to(outgoing[:, None], (experts, 2, capacity, breadth)).reshape(
        wide_count, narrow_count, capacity, breadth
    )
    arrived = lax.all_to_all(
        lax.all_to_all(doubled, "wide", split_axis=0, concat_axis=0, tiled=True),
        "narrow",
        split_axis=1,
        concat_axis=1,
        tiled=True,
    )
    gate_dense = dequantize(gate_codes[0], gate_scale[0])
    up_dense = dequantize(up_codes[0], up_scale[0])
    down_dense = dequantize(down_codes[0], down_scale[0])
    produced = swiglu(arrived.reshape(-1, breadth), gate_dense, up_dense, down_dense)
    produced = produced.reshape(wide_count, narrow_count, capacity, breadth)
    returned = lax.all_to_all(
        lax.all_to_all(produced, "wide", split_axis=0, concat_axis=0, tiled=True),
        "narrow",
        split_axis=1,
        concat_axis=1,
        tiled=True,
    )
    paired = returned.reshape(experts, 2, capacity, breadth)
    summed = paired[:, 0].astype(jnp.float32) + paired[:, 1].astype(jnp.float32)
    combine = placing.astype(jnp.float32) * jnp.transpose(weight_of)[:, None, :]
    routed = jnp.einsum("ecr,ecd->rd", combine, summed, precision=lax.Precision.HIGHEST)
    thinker_out = (residual + routed).astype(jnp.bfloat16)
    own_wide = talker_source // row_count // narrow_count
    own_local = talker_source % row_count
    gathered = lax.all_gather(thinker_out, "wide", axis=0, tiled=True)
    talker_in = jnp.take(gathered, own_wide * row_count + own_local, axis=0)
    talker_normed = rms_norm(talker_in, talker_gain)
    talk_capacity = min(row_count, max(2, 2 * row_count * TTOP // narrow_count))
    talk_placing, talk_weight = slot_tables(talk_ids, talk_gates, narrow_count, talk_capacity)
    talk_outgoing = jnp.einsum(
        "ecr,rd->ecd",
        talk_placing.astype(jnp.bfloat16),
        talker_normed,
        preferred_element_type=jnp.float32,
    ).astype(jnp.bfloat16)
    incoming = lax.all_to_all(talk_outgoing, "narrow", split_axis=0, concat_axis=0, tiled=True)
    sources = incoming.shape[0]
    items = incoming.shape[1]
    result = swiglu(incoming.reshape(-1, breadth), talk_gate_w[0], talk_up_w[0], talk_down_w[0])
    talk_done = result.reshape(sources, items, -1)
    talk_back = lax.all_to_all(talk_done, "narrow", split_axis=0, concat_axis=0, tiled=True)
    talk_combine = talk_placing.astype(jnp.float32) * jnp.transpose(talk_weight)[:, None, :]
    talked = jnp.einsum(
        "ecr,ecd->rd", talk_combine, talk_back.astype(jnp.float32), precision=lax.Precision.HIGHEST
    )
    return (thinker_out, talked.astype(jnp.bfloat16))


EXT = 128
MESH = pl.DeviceIdType.MESH


def attention(
    hidden, queries, keys, values, new_key, new_value, lengths_ref, gain, asked, scores, mixture, residual, before_values
):
    rows, breadth = residual.shape
    for head in range(HEADS):
        asked[:, head, :] = queries[:, head * HEAD_DIM : (head + 1) * HEAD_DIM].astype(jnp.float32)
    scaling = HEAD_DIM ** (-0.5)
    lower = lax.broadcasted_iota(jnp.int32, (HEADS, HEAD_DIM), 0) < HEADS // KV_HEADS
    places = lax.broadcasted_iota(jnp.int32, (HEADS, HEAD_DIM), 1)
    contract = (((1,), (1,)), ((), ()))
    fresh = []
    for row in range(rows):
        query = asked[row]
        packed = query.astype(jnp.bfloat16)
        first = lax.dot_general(packed, keys[row, :, :HEAD_DIM], contract, preferred_element_type=jnp.float32)
        second = lax.dot_general(packed, keys[row, :, HEAD_DIM:], contract, preferred_element_type=jnp.float32)
        found = jnp.where(lower, first, second) * scaling
        scores[row] = jnp.where(places < lengths_ref[row], found, -jnp.inf)
        newest = jnp.where(
            lower,
            new_key[row : row + 1, :HEAD_DIM].astype(jnp.float32),
            new_key[row : row + 1, HEAD_DIM:].astype(jnp.float32),
        )
        fresh.append(jnp.sum(query * newest, axis=1, keepdims=True) * scaling)
    before_values()
    for row in range(rows):
        found = scores[row]
        highest = jnp.maximum(jnp.max(found, axis=1, keepdims=True), fresh[row])
        weights = jnp.exp(found - highest)
        own_weight = jnp.exp(fresh[row] - highest)
        totals = jnp.sum(weights, axis=1, keepdims=True) + own_weight
        probabilities = (weights / totals).astype(jnp.bfloat16)
        own_prob = (own_weight / totals).astype(jnp.bfloat16).astype(jnp.float32)
        first = jnp.dot(probabilities, values[row, :, :HEAD_DIM], preferred_element_type=jnp.float32)
        second = jnp.dot(probabilities, values[row, :, HEAD_DIM:], preferred_element_type=jnp.float32)
        newest = jnp.where(
            lower,
            new_value[row : row + 1, :HEAD_DIM].astype(jnp.float32),
            new_value[row : row + 1, HEAD_DIM:].astype(jnp.float32),
        )
        mixture[row] = jnp.where(lower, first, second) + own_prob * newest
    square = jnp.zeros((rows, HEAD_DIM), jnp.float32)
    for head in range(HEADS):
        columns = slice(head * HEAD_DIM, (head + 1) * HEAD_DIM)
        part = hidden[:, columns].astype(jnp.float32) + mixture[:, head, :]
        residual[:, columns] = part
        square = square + part * part
    factor = lax.rsqrt(jnp.sum(square, axis=1, keepdims=True) / breadth + EPSILON)
    normed = []
    for head in range(HEADS):
        part = residual[:, head * HEAD_DIM : (head + 1) * HEAD_DIM] * factor
        normed.append((part * gain[head : head + 1, :].astype(jnp.float32)).astype(jnp.bfloat16))
    return normed


def layer_kernel(
    lengths_ref, source_ref, gate_scale_ref, up_scale_ref, down_scale_ref, key_hbm, queries_hbm, new_key_hbm, value_hbm,
    new_value_hbm, hidden_hbm, gain_hbm, ids_hbm, gates_hbm, talk_ids_hbm, talk_gates_hbm, gate_hbm, up_hbm, down_hbm,
    talker_gain_hbm, talk_gate_hbm, talk_up_hbm, talk_down_hbm,
    thinker_ref, talker_ref,
    keys, queries, new_key, values, new_value, hidden, gain, ids, gates, talk_ids, talk_gates, gate_w, up_w, down_w,
    talker_gain, talk_gate_w, talk_up_w, talk_down_w, load_sem, asked, scores, mixture, residual,
    rows_a, rows_b, kept, core_out, core_in, y_out, y_in, x_out, x_in, x_late_out, x_late_in, y_late_out, y_late_in,
    z_out, z_in, meta_out, meta_in, meta_rows, talk_rows, spaced, talk_out, talk_in, send_sem, recv_sem,
):
    f32, bf16 = jnp.float32, jnp.bfloat16
    wide, narrow = lax.axis_index("wide"), lax.axis_index("narrow")
    z, x, y, c = wide // 2, wide % 2, narrow // 2, narrow % 2
    half = 1024

    def peer(dz, bx, by, bc):
        there = (z + dz) % 4 if dz else z
        return (there * 2 + (1 - x if bx else x), (1 - y if by else y) * 2 + (1 - c if bc else c))

    loads = []
    for number, (source, target) in enumerate((
        (key_hbm, keys), (queries_hbm, queries), (new_key_hbm, new_key), (value_hbm, values),
        (new_value_hbm, new_value), (hidden_hbm, hidden), (gain_hbm, gain), (ids_hbm, ids), (gates_hbm, gates),
        (talk_ids_hbm, talk_ids), (talk_gates_hbm, talk_gates), (gate_hbm.at[0], gate_w), (up_hbm.at[0], up_w),
        (down_hbm.at[0], down_w), (talker_gain_hbm, talker_gain), (talk_gate_hbm.at[0], talk_gate_w),
        (talk_up_hbm.at[0], talk_up_w), (talk_down_hbm.at[0], talk_down_w),
    )):
        load = pltpu.make_async_copy(source, target, load_sem.at[number])
        load.start()
        loads.append(load)
    barrier = pltpu.get_barrier_semaphore()
    everyone = [
        (dz, bx, by, bc) for dz in range(4) for bx in range(2) for by in range(2) for bc in range(2) if dz or bx or by or bc
    ]
    for one in everyone:
        pl.semaphore_signal(barrier, inc=1, device_id=peer(*one), device_id_type=MESH)

    down_iota = lax.broadcasted_iota(jnp.int32, (16, 16), 0)
    along_iota = lax.broadcasted_iota(jnp.int32, (16, 16), 1)
    rel_down, rel_along, origin = (jnp.zeros((16, 16), jnp.int32) for _ in range(3))
    for position in range(16):
        number = source_ref[position]
        from_wide = lax.div(number, 64)
        from_z, from_x = lax.div(from_wide, 2), lax.rem(from_wide, 2)
        relative = lax.rem(from_z - z + 4, 4) * 2 + lax.rem(from_x + x, 2)
        rel_down = jnp.where(down_iota == position, relative, rel_down)
        rel_along = jnp.where(along_iota == position, relative, rel_along)
        origin = jnp.where(along_iota == position, lax.rem(number, 16), origin)
    same = rel_down == rel_along
    rank_down = jnp.sum(jnp.where(same & (along_iota < down_iota), 1.0, 0.0), axis=1, keepdims=True)
    rank_along = jnp.sum(jnp.where(same & (down_iota < along_iota), 1.0, 0.0), axis=0, keepdims=True)
    slot_down = rel_down.astype(f32) * 2 + rank_down
    slot_along = rel_along.astype(f32) * 2 + rank_along
    place = jnp.where(slot_down == along_iota.astype(f32), 1.0, 0.0).astype(bf16)
    place_across = jnp.where(slot_along == down_iota.astype(f32), 1.0, 0.0).astype(bf16)
    identity = jnp.where(down_iota == along_iota, 1.0, 0.0).astype(bf16)
    contract = (((1,), (1,)), ((), ()))
    lines = lax.broadcasted_iota(jnp.int32, (EXT, 16), 0)
    for number in range(7, 11):
        loads[number].wait()
    weight = jnp.zeros((EXT, 16), f32)
    for choice in range(TOP):
        weight = weight + jnp.where(ids[choice : choice + 1, :] == lines % 16, gates[choice : choice + 1, :], 0.0)
    high = weight.astype(bf16).astype(f32)
    split = jnp.where(lines < 16, high, weight - high).astype(bf16)
    extras = lax.dot_general(identity, split, contract, preferred_element_type=f32).astype(bf16)
    weight = jnp.zeros((EXT, 16), f32)
    for choice in range(TTOP):
        weight = weight + jnp.where(
            talk_ids[choice : choice + 1, :] == lines % 8, talk_gates[choice : choice + 1, :], 0.0
        )
    high = weight.astype(bf16).astype(f32)
    split = jnp.where(lines < 8, high, weight - high)
    split = jnp.where(lines == 4, origin[0:1, :].astype(f32), split).astype(bf16)
    by_slot = lax.dot_general(place_across, split, contract, preferred_element_type=f32)
    meta_out[...] = jnp.zeros_like(meta_out)
    for slot in range(8):
        meta_out[slot, 0:2, :] = by_slot[2 * slot : 2 * slot + 2, :]
    meta_in[0] = meta_out[0]

    for number in range(3):
        loads[number].wait()

    def before_values():
        for number in range(3, 7):
            loads[number].wait()

    normed = attention(
        hidden, queries, keys, values, new_key, new_value, lengths_ref, gain, asked, scores, mixture, residual,
        before_values,
    )
    for head in range(8):
        columns = slice(head * HEAD_DIM, (head + 1) * HEAD_DIM)
        rows_a[0, 0, :, columns] = normed[head]
        rows_b[0, 0, :, columns] = normed[8 + head]
    rows_a[0, 0, :, half:] = extras
    pl.semaphore_wait(barrier, len(everyone))

    pending = []

    def send(source, target, to):
        number = len(pending)
        copy = pltpu.make_async_remote_copy(
            src_ref=source, dst_ref=target, send_sem=send_sem.at[number], recv_sem=recv_sem.at[number],
            device_id=peer(*to), device_id_type=MESH,
        )
        copy.start()
        pending.append(copy)
        return copy

    to_x, to_y, to_c = (0, 1, 0, 0), (0, 0, 1, 0), (0, 0, 0, 1)
    a_x = [send(rows_a.at[0, 0], rows_a.at[2, 0], to_x)]
    b_y = [send(rows_b.at[0, 0], rows_b.at[4, 0], to_y)]
    a_z, b_z = {}, {}
    for step in (2, 1, 3):
        a_z[step] = send(rows_a.at[0, 0], rows_a.at[0, 4 - step], (step, 0, 0, 0))
        b_z[step] = send(rows_b.at[0, 0], rows_b.at[0, 4 - step], (step, 0, 0, 0))
    a_y = [send(rows_a.at[0, 0], rows_a.at[4, 0], to_y)]
    b_x = [send(rows_b.at[0, 0], rows_b.at[2, 0], to_x)]
    meta_copies = []
    for dz in range(4):
        for bx in range(2):
            if dz or bx:
                meta_copies.append(
                    send(meta_out.at[dz * 2 + bx], meta_in.at[(4 - dz) % 4 * 2 + bx], (dz, bx, 0, 0))
                )

    def scaled(weights, scale, row_block, column_blocks):
        rows = pl.ds(pl.multiple_of(row_block * BLK, BLK), BLK)
        for column in range(column_blocks):
            columns = slice(column * BLK, (column + 1) * BLK)
            weights[rows, columns] = (weights[rows, columns].astype(f32) * scale(row_block, column)).astype(bf16)

    loads[11].wait()
    loads[12].wait()

    def scale_inner(first, last):
        def body(row_block, carry):
            scaled(gate_w, lambda i, j: gate_scale_ref[j, 0, i], row_block, 3)
            scaled(up_w, lambda i, j: up_scale_ref[j, 0, i], row_block, 3)
            return carry

        lax.fori_loop(first, last, body, 0)

    scale_inner(0, 4)
    for step in (1, 3, 2):
        rel = 4 - step
        a_z[step].wait_recv()
        a_x.append(send(rows_a.at[0, rel], rows_a.at[2, rel], to_x))
        b_z[step].wait_recv()
        b_y.append(send(rows_b.at[0, rel], rows_b.at[4, rel], to_y))
        a_y.append(send(rows_a.at[0, rel], rows_a.at[4, rel], to_y))
        b_x.append(send(rows_b.at[0, rel], rows_b.at[2, rel], to_x))
    across = [send(rows_a.at[0], rows_a.at[1], to_c), send(rows_b.at[0], rows_b.at[1], to_c)]
    a_far, b_far = [], []
    for number, rel in enumerate((0, 3, 1, 2)):
        a_x[number].wait_recv()
        a_far.append(send(rows_a.at[2, rel], rows_a.at[6, rel], to_y))
        b_y[number].wait_recv()
        b_far.append(send(rows_b.at[4, rel], rows_b.at[6, rel], to_x))
        if number < 3:
            scale_inner(4 + number * 4, 8 + number * 4)
    across += [send(rows_a.at[2], rows_a.at[3], to_c), send(rows_b.at[4], rows_b.at[5], to_c)]
    loads[13].wait()

    def scale_outer(row_block, carry):
        scaled(down_w, lambda i, j: down_scale_ref[i, 0, j], row_block, 16)
        return carry

    lax.fori_loop(0, 3, scale_outer, 0)
    def weight_column(extras, first, second):
        lanes = lax.broadcasted_iota(jnp.int32, extras.shape, 1)
        return jnp.sum(jnp.where((lanes == first) | (lanes == second), extras.astype(f32), 0.0), axis=1, keepdims=True)

    expert = wide * 2 + narrow // 2

    def hidden_units(first, count):
        base, count = 2 * first, 2 * count
        left = rows_a[base : base + count].reshape(count * 64, half + EXT)
        right = rows_b[base : base + count].reshape(count * 64, half)
        weight = weight_column(left[:, half:], expert, expert + 16)
        left = left[:, :half]
        gated = jnp.dot(left, gate_w[:half], preferred_element_type=f32)
        gated = gated + jnp.dot(right, gate_w[half:], preferred_element_type=f32)
        lifted = jnp.dot(left, up_w[:half], preferred_element_type=f32)
        lifted = lifted + jnp.dot(right, up_w[half:], preferred_element_type=f32)
        return (jax.nn.silu(gated) * lifted).astype(bf16), weight

    core_copies = {}

    def process(first, count):
        middle, weight = hidden_units(first, count)
        for column in range(4):
            columns = slice(column * 512, (column + 1) * 512)
            part = jnp.dot(middle, down_w[:, columns], preferred_element_type=f32) * weight
            for at in range(count):
                kept[first + at, :, columns] = part[at * 128 : at * 128 + 64]
                core_out[first + at, :, columns] = part[at * 128 + 64 : at * 128 + 128].astype(bf16)
        for group in range(first, first + count):
            core_copies[group] = send(core_out.at[group], core_in.at[group], to_c)

    across[0].wait_recv()
    across[1].wait_recv()
    process(0, 1)
    for copy in a_y + b_x:
        copy.wait_recv()
    across += [send(rows_a.at[4], rows_a.at[5], to_c), send(rows_b.at[2], rows_b.at[3], to_c)]
    for copy in across[2:]:
        copy.wait_recv()
    process(1, 2)
    for copy in a_far + b_far:
        copy.wait_recv()
    across_far = [send(rows_a.at[6], rows_a.at[7], to_c), send(rows_b.at[6], rows_b.at[7], to_c)]
    for group in range(3):
        core_copies[group].wait_recv()
        kept[group] = kept[group] + core_in[group].astype(f32)
    for rel in range(4):
        y_out[0, rel] = kept[2, rel * 16 : (rel + 1) * 16, :half].astype(bf16)
        x_out[0, rel] = kept[1, rel * 16 : (rel + 1) * 16, half:].astype(bf16)
    near = [send(y_out.at[0], y_in.at[0], to_y), send(x_out.at[0], x_in.at[0], to_x)]
    for copy in across_far:
        copy.wait_recv()
    process(3, 1)
    core_copies[3].wait_recv()
    order = (2, 1, 3, 0)
    first_y, first_x = {}, {}
    for rel in order:
        span = slice(rel * 16, (rel + 1) * 16)
        y_out[1, rel] = (kept[3, span, :half] + core_in[3, span, :half].astype(f32)).astype(bf16)
        x_out[1, rel] = (kept[3, span, half:] + core_in[3, span, half:].astype(f32)).astype(bf16)
        first_y[rel] = send(y_out.at[1, rel], y_in.at[1, rel], to_y)
        first_x[rel] = send(x_out.at[1, rel], x_in.at[1, rel], to_x)
    late_x, late_y = {}, {}
    for rel in order:
        span = slice(rel * 16, (rel + 1) * 16)
        first_y[rel].wait_recv()
        x_late_out[rel] = (kept[1, span, :half] + y_in[1, rel].astype(f32)).astype(bf16)
        late_x[rel] = send(x_late_out.at[rel], x_late_in.at[rel], to_x)
        first_x[rel].wait_recv()
        y_late_out[rel] = (kept[2, span, half:] + x_in[1, rel].astype(f32)).astype(bf16)
        late_y[rel] = send(y_late_out.at[rel], y_late_in.at[rel], to_y)
    for copy in near:
        copy.wait_recv()
    z_copies = {}
    for rel in order:
        span = slice(rel * 16, (rel + 1) * 16)
        late_x[rel].wait_recv()
        late_y[rel].wait_recv()
        left = kept[0, span, :half] + y_in[0, rel].astype(f32) + x_late_in[rel].astype(f32)
        right = kept[0, span, half:] + x_in[0, rel].astype(f32) + y_late_in[rel].astype(f32)
        if rel:
            z_out[rel, :, :half] = left.astype(bf16)
            z_out[rel, :, half:] = right.astype(bf16)
            z_copies[rel] = send(z_out.at[rel], z_in.at[4 - rel], (rel, 0, 0, 0))
    sums = [left[:, :512], left[:, 512:], right[:, :512], right[:, 512:]]
    for rel in (1, 2, 3):
        z_copies[rel].wait_recv()
    for copy in meta_copies:
        copy.wait_recv()
    for load in loads[14:]:
        load.wait()
    square = jnp.zeros((16, 512), f32)
    finals = []
    for column in range(4):
        span = slice(column * 512, (column + 1) * 512)
        total = residual[:, span] + sums[column]
        for rel in (1, 2, 3):
            total = total + z_in[rel, :, span].astype(f32)
        final = total.astype(bf16)
        thinker_ref[:, span] = final
        final = final.astype(f32)
        finals.append(final)
        square = square + final * final
    factor = lax.rsqrt(jnp.sum(square, axis=1, keepdims=True) / 2048 + EPSILON)
    for slot in range(8):
        meta_rows[2 * slot : 2 * slot + 2, :] = meta_in[slot, 0:2, :]
    meta = meta_rows[...]
    picks = (meta[:, 4:5].astype(jnp.int32) == lax.broadcasted_iota(jnp.int32, (16, 16), 1)).astype(f32).astype(bf16)
    for column in range(4):
        span = slice(column * 512, (column + 1) * 512)
        for block in range(4):
            row = column * 4 + block
            normed = finals[column][:, block * BLK : (block + 1) * BLK] * factor
            normed = (normed * talker_gain[row : row + 1, :].astype(f32)).astype(bf16)
            talk_rows[0, :, row * BLK : (row + 1) * BLK] = jnp.dot(picks, normed, preferred_element_type=f32).astype(bf16)
    talk_rows[0, :, 2048:] = meta.astype(bf16)
    gathers = [send(talk_rows.at[0], talk_rows.at[v], (0, 0, v // 2, v % 2)) for v in (3, 2, 1)]
    for copy in gathers:
        copy.wait_recv()
    inputs = talk_rows[...].reshape(64, 2048 + EXT)
    weight = weight_column(inputs[:, 2048:], narrow, narrow + 8)
    inputs = inputs[:, :2048]
    gated = jnp.dot(inputs, talk_gate_w[...], preferred_element_type=f32)
    lifted = jnp.dot(inputs, talk_up_w[...], preferred_element_type=f32)
    middle = (jax.nn.silu(gated) * lifted).astype(bf16)
    result = jnp.dot(middle, talk_down_w[...], preferred_element_type=f32) * weight
    for column in range(8):
        spaced[:, column, :] = result[:, column * 128 : (column + 1) * 128]
    talk_out[...] = spaced[...].reshape(512, 128).astype(bf16).reshape(4, 8, 16, 128)
    backs = []
    for dz in (2, 1, 3, 0):
        for bx in range(2):
            for v in range(4):
                if dz or bx or v:
                    backs.append(
                        send(
                            talk_out.at[v, dz * 2 + bx], talk_in.at[v, (4 - dz) % 4 * 2 + bx], (dz, bx, v // 2, v % 2)
                        )
                    )
    talk_in[0, 0] = talk_out[0, 0]
    for copy in backs:
        copy.wait_recv()
    total = talk_in[0].astype(f32)
    for v in range(1, 4):
        total = total + talk_in[v].astype(f32)
    spaced[:16] = total.reshape(16, 8, 128)
    for column in range(8):
        part = spaced[:16, column, :].astype(bf16)
        talker_ref[:, column * 128 : (column + 1) * 128] = jnp.dot(
            place, part, preferred_element_type=f32
        ).astype(bf16)
    for copy in pending:
        copy.wait_send()


def local_fused(
    hidden_in, queries, cache_key, cache_value, new_key, new_value, lengths, norm_gain, gate_codes, gate_scale,
    up_codes, up_scale, down_codes, down_scale, think_ids, think_gates, talker_source, talker_gain, talk_gate_w,
    talk_up_w, talk_down_w, talk_ids, talk_gates,
):
    f32, bf16 = jnp.float32, jnp.bfloat16
    vmem, smem, hbm = (pl.BlockSpec(memory_space=s) for s in (pltpu.VMEM, pltpu.SMEM, pltpu.HBM))
    operands = [
        lengths, talker_source, jnp.transpose(gate_scale, (2, 0, 1)), jnp.transpose(up_scale, (2, 0, 1)),
        jnp.transpose(down_scale, (1, 0, 2)), cache_key, queries, new_key, cache_value, new_value, hidden_in,
        norm_gain.reshape(16, 128), think_ids.T, think_gates.T, talk_ids.T, talk_gates.T, gate_codes, up_codes,
        down_codes, talker_gain.reshape(16, 128), talk_gate_w, talk_up_w, talk_down_w,
    ]
    landing = []
    for operand in operands[5:]:
        shape = operand.shape[1:] if operand.shape[0] == 1 else operand.shape
        landing.append(pltpu.VMEM(shape, operand.dtype))
    rows, breadth = hidden_in.shape
    return pl.pallas_call(
        layer_kernel,
        out_shape=(jax.ShapeDtypeStruct((rows, breadth), bf16), jax.ShapeDtypeStruct((rows, 1024), bf16)),
        in_specs=[smem] * 5 + [hbm] * 18,
        out_specs=(vmem, vmem),
        scratch_shapes=landing
        + [
            pltpu.SemaphoreType.DMA((18,)),
            pltpu.VMEM((rows, HEADS, HEAD_DIM), f32),
            pltpu.VMEM((rows, HEADS, HEAD_DIM), f32),
            pltpu.VMEM((rows, HEADS, HEAD_DIM), f32),
            pltpu.VMEM((rows, breadth), f32),
            pltpu.VMEM((8, 4, 16, 1024 + EXT), bf16),
            pltpu.VMEM((8, 4, 16, 1024), bf16),
            pltpu.VMEM((4, 64, 2048), f32),
            pltpu.VMEM((4, 64, 2048), bf16),
            pltpu.VMEM((4, 64, 2048), bf16),
            pltpu.VMEM((2, 4, 16, 1024), bf16),
            pltpu.VMEM((2, 4, 16, 1024), bf16),
            pltpu.VMEM((2, 4, 16, 1024), bf16),
            pltpu.VMEM((2, 4, 16, 1024), bf16),
            pltpu.VMEM((4, 16, 1024), bf16),
            pltpu.VMEM((4, 16, 1024), bf16),
            pltpu.VMEM((4, 16, 1024), bf16),
            pltpu.VMEM((4, 16, 1024), bf16),
            pltpu.VMEM((4, 16, 2048), bf16),
            pltpu.VMEM((4, 16, 2048), bf16),
            pltpu.VMEM((8, 8, EXT), f32),
            pltpu.VMEM((8, 8, EXT), f32),
            pltpu.VMEM((16, EXT), f32),
            pltpu.VMEM((4, 16, 2048 + EXT), bf16),
            pltpu.VMEM((64, 8, 128), f32),
            pltpu.VMEM((4, 8, 16, 128), bf16),
            pltpu.VMEM((4, 8, 16, 128), bf16),
            pltpu.SemaphoreType.DMA((112,)),
            pltpu.SemaphoreType.DMA((112,)),
        ],
        compiler_params=pltpu.CompilerParams(
            collective_id=0, has_side_effects=True, vmem_limit_bytes=48 * 2**20
        ),
    )(*operands)


def solution(mesh):
    return jax.shard_map(
        local_fused if mesh.shape["wide"] == 8 and mesh.shape["narrow"] == 4 else local,
        mesh=mesh,
        in_specs=(
            P(("wide", "narrow"), None),
            P(("wide", "narrow"), None),
            P(("wide", "narrow"), None, None),
            P(("wide", "narrow"), None, None),
            P(("wide", "narrow"), None),
            P(("wide", "narrow"), None),
            P(("wide", "narrow")),
            P(),
            P(("wide", "narrow"), None, None),
            P(("wide", "narrow"), None, None),
            P(("wide", "narrow"), None, None),
            P(("wide", "narrow"), None, None),
            P(("wide", "narrow"), None, None),
            P(("wide", "narrow"), None, None),
            P(("wide", "narrow"), None),
            P(("wide", "narrow"), None),
            P(("wide", "narrow")),
            P(),
            P("narrow", None, None),
            P("narrow", None, None),
            P("narrow", None, None),
            P(("wide", "narrow"), None),
            P(("wide", "narrow"), None),
        ),
        out_specs=(P(("wide", "narrow"), None), P(("wide", "narrow"), None)),
        check_vma=False,
    )
```

```python
import jax
import jax.numpy as jnp
from jax import lax
from jax.experimental import pallas as pl
from jax.experimental.pallas import tpu as pltpu
from jax.sharding import PartitionSpec as P

HEADS = 16
KV_HEADS = 2
HEAD_DIM = 128
BLK = 128
TOP = 8
TTOP = 2


EPSILON = 1e-06


def dequantize(code_block, scale_block):
    height, breadth = code_block.shape
    tiles = code_block.astype(jnp.float32).reshape(height // BLK, BLK, breadth // BLK, BLK)
    tiles = tiles * scale_block[:, None, :, None]
    return tiles.reshape(height, breadth).astype(jnp.bfloat16)


def rms_norm(values, gain):
    values = values.astype(jnp.float32)
    spread = jnp.mean(values * values, axis=-1, keepdims=True)
    return (values * lax.rsqrt(spread + EPSILON) * gain.astype(jnp.float32)).astype(jnp.bfloat16)


def swiglu(inputs, gate_dense, up_dense, down_dense):
    gated = jnp.dot(inputs, gate_dense, preferred_element_type=jnp.float32)
    lifted = jnp.dot(inputs, up_dense, preferred_element_type=jnp.float32)
    middle = (jax.nn.silu(gated) * lifted).astype(jnp.bfloat16)
    return jnp.dot(middle, down_dense, preferred_element_type=jnp.float32).astype(jnp.bfloat16)


def attend(queries, cache_key, cache_value, new_key, new_value, lengths):
    row_count = queries.shape[0]
    positions = cache_key.shape[1]
    groups = HEADS // KV_HEADS
    scaling = HEAD_DIM ** (-0.5)
    asked = queries.reshape(row_count, KV_HEADS, groups, HEAD_DIM)
    cached_keys = cache_key.reshape(row_count, positions, KV_HEADS, HEAD_DIM)
    cached_values = cache_value.reshape(row_count, positions, KV_HEADS, HEAD_DIM)
    scores = (
        jnp.einsum("rkgd,rtkd->rkgt", asked, cached_keys, preferred_element_type=jnp.float32)
        * scaling
    )
    newest_key = new_key.reshape(row_count, KV_HEADS, HEAD_DIM)
    fresh_score = (
        jnp.einsum("rkgd,rkd->rkg", asked, newest_key, preferred_element_type=jnp.float32) * scaling
    )
    places = jnp.arange(positions, dtype=jnp.int32)
    live_mask = places[None, :] < lengths[:, None]
    scores = jnp.where(live_mask[:, None, None, :], scores, -jnp.inf)
    highest = jnp.maximum(jnp.max(scores, axis=-1), fresh_score)
    weights = jnp.exp(scores - highest[..., None])
    own_weight = jnp.exp(fresh_score - highest)
    totals = jnp.sum(weights, axis=-1) + own_weight
    probabilities = (weights / totals[..., None]).astype(jnp.bfloat16)
    own_prob = (own_weight / totals).astype(jnp.bfloat16)
    mixture = jnp.einsum(
        "rkgt,rtkd->rkgd", probabilities, cached_values, preferred_element_type=jnp.float32
    )
    newest = new_value.reshape(row_count, KV_HEADS, 1, HEAD_DIM).astype(jnp.float32)
    mixture = mixture + own_prob.astype(jnp.float32)[..., None] * newest
    return mixture.reshape(row_count, HEADS * HEAD_DIM)


def slot_tables(expert_ids, gate_weights, expert_count, capacity):
    chosen = expert_ids[:, :, None] == jnp.arange(expert_count, dtype=jnp.int32)[None, None, :]
    picked = jnp.any(chosen, axis=1).astype(jnp.int32)
    weight_of = jnp.sum(jnp.where(chosen, gate_weights[:, :, None], jnp.float32(0.0)), axis=1)
    ranks = jnp.cumsum(picked, axis=0) - picked
    onehot = (picked[:, :, None] == 1) & (
        ranks[:, :, None] == jnp.arange(capacity, dtype=jnp.int32)[None, None, :]
    )
    placing = jnp.transpose(onehot, (1, 2, 0))
    return (placing, weight_of)


def local(
    hidden_in,
    queries,
    cache_key,
    cache_value,
    new_key,
    new_value,
    lengths,
    norm_gain,
    gate_codes,
    gate_scale,
    up_codes,
    up_scale,
    down_codes,
    down_scale,
    think_ids,
    think_gates,
    talker_source,
    talker_gain,
    talk_gate_w,
    talk_up_w,
    talk_down_w,
    talk_ids,
    talk_gates,
):
    wide_count = lax.axis_size("wide")
    narrow_count = lax.axis_size("narrow")
    row_count = hidden_in.shape[0]
    breadth = hidden_in.shape[1]
    attended = attend(queries, cache_key, cache_value, new_key, new_value, lengths)
    residual = hidden_in.astype(jnp.float32) + attended
    normed = rms_norm(residual, norm_gain)
    experts = wide_count * narrow_count // 2
    capacity = min(row_count, max(2, 2 * row_count * TOP // experts))
    placing, weight_of = slot_tables(think_ids, think_gates, experts, capacity)
    outgoing = jnp.einsum(
        "ecr,rd->ecd", placing.astype(jnp.bfloat16), normed, preferred_element_type=jnp.float32
    ).astype(jnp.bfloat16)
    doubled = jnp.broadcast_to(outgoing[:, None], (experts, 2, capacity, breadth)).reshape(
        wide_count, narrow_count, capacity, breadth
    )
    arrived = lax.all_to_all(
        lax.all_to_all(doubled, "wide", split_axis=0, concat_axis=0, tiled=True),
        "narrow",
        split_axis=1,
        concat_axis=1,
        tiled=True,
    )
    gate_dense = dequantize(gate_codes[0], gate_scale[0])
    up_dense = dequantize(up_codes[0], up_scale[0])
    down_dense = dequantize(down_codes[0], down_scale[0])
    produced = swiglu(arrived.reshape(-1, breadth), gate_dense, up_dense, down_dense)
    produced = produced.reshape(wide_count, narrow_count, capacity, breadth)
    returned = lax.all_to_all(
        lax.all_to_all(produced, "wide", split_axis=0, concat_axis=0, tiled=True),
        "narrow",
        split_axis=1,
        concat_axis=1,
        tiled=True,
    )
    paired = returned.reshape(experts, 2, capacity, breadth)
    summed = paired[:, 0].astype(jnp.float32) + paired[:, 1].astype(jnp.float32)
    combine = placing.astype(jnp.float32) * jnp.transpose(weight_of)[:, None, :]
    routed = jnp.einsum("ecr,ecd->rd", combine, summed, precision=lax.Precision.HIGHEST)
    thinker_out = (residual + routed).astype(jnp.bfloat16)
    own_wide = talker_source // row_count // narrow_count
    own_local = talker_source % row_count
    gathered = lax.all_gather(thinker_out, "wide", axis=0, tiled=True)
    talker_in = jnp.take(gathered, own_wide * row_count + own_local, axis=0)
    talker_normed = rms_norm(talker_in, talker_gain)
    talk_capacity = min(row_count, max(2, 2 * row_count * TTOP // narrow_count))
    talk_placing, talk_weight = slot_tables(talk_ids, talk_gates, narrow_count, talk_capacity)
    talk_outgoing = jnp.einsum(
        "ecr,rd->ecd",
        talk_placing.astype(jnp.bfloat16),
        talker_normed,
        preferred_element_type=jnp.float32,
    ).astype(jnp.bfloat16)
    incoming = lax.all_to_all(talk_outgoing, "narrow", split_axis=0, concat_axis=0, tiled=True)
    sources = incoming.shape[0]
    items = incoming.shape[1]
    result = swiglu(incoming.reshape(-1, breadth), talk_gate_w[0], talk_up_w[0], talk_down_w[0])
    talk_done = result.reshape(sources, items, -1)
    talk_back = lax.all_to_all(talk_done, "narrow", split_axis=0, concat_axis=0, tiled=True)
    talk_combine = talk_placing.astype(jnp.float32) * jnp.transpose(talk_weight)[:, None, :]
    talked = jnp.einsum(
        "ecr,ecd->rd", talk_combine, talk_back.astype(jnp.float32), precision=lax.Precision.HIGHEST
    )
    return (thinker_out, talked.astype(jnp.bfloat16))


EXT = 128
MESH = pl.DeviceIdType.MESH


def attention(
    hidden, queries, keys, values, new_key, new_value, lengths_ref, gain, asked, scores, mixture, residual, before_values
):
    rows, breadth = residual.shape
    for head in range(HEADS):
        asked[:, head, :] = queries[:, head * HEAD_DIM : (head + 1) * HEAD_DIM].astype(jnp.float32)
    scaling = HEAD_DIM ** (-0.5)
    lower = lax.broadcasted_iota(jnp.int32, (HEADS, HEAD_DIM), 0) < HEADS // KV_HEADS
    places = lax.broadcasted_iota(jnp.int32, (HEADS, HEAD_DIM), 1)
    contract = (((1,), (1,)), ((), ()))
    fresh = []
    for row in range(rows):
        query = asked[row]
        packed = query.astype(jnp.bfloat16)
        first = lax.dot_general(packed, keys[row, :, :HEAD_DIM], contract, preferred_element_type=jnp.float32)
        second = lax.dot_general(packed, keys[row, :, HEAD_DIM:], contract, preferred_element_type=jnp.float32)
        found = jnp.where(lower, first, second) * scaling
        scores[row] = jnp.where(places < lengths_ref[row], found, -jnp.inf)
        newest = jnp.where(
            lower,
            new_key[row : row + 1, :HEAD_DIM].astype(jnp.float32),
            new_key[row : row + 1, HEAD_DIM:].astype(jnp.float32),
        )
        fresh.append(jnp.sum(query * newest, axis=1, keepdims=True) * scaling)
    before_values()
    for row in range(rows):
        found = scores[row]
        highest = jnp.maximum(jnp.max(found, axis=1, keepdims=True), fresh[row])
        weights = jnp.exp(found - highest)
        own_weight = jnp.exp(fresh[row] - highest)
        totals = jnp.sum(weights, axis=1, keepdims=True) + own_weight
        probabilities = (weights / totals).astype(jnp.bfloat16)
        own_prob = (own_weight / totals).astype(jnp.bfloat16).astype(jnp.float32)
        first = jnp.dot(probabilities, values[row, :, :HEAD_DIM], preferred_element_type=jnp.float32)
        second = jnp.dot(probabilities, values[row, :, HEAD_DIM:], preferred_element_type=jnp.float32)
        newest = jnp.where(
            lower,
            new_value[row : row + 1, :HEAD_DIM].astype(jnp.float32),
            new_value[row : row + 1, HEAD_DIM:].astype(jnp.float32),
        )
        mixture[row] = jnp.where(lower, first, second) + own_prob * newest
    square = jnp.zeros((rows, HEAD_DIM), jnp.float32)
    for head in range(HEADS):
        columns = slice(head * HEAD_DIM, (head + 1) * HEAD_DIM)
        part = hidden[:, columns].astype(jnp.float32) + mixture[:, head, :]
        residual[:, columns] = part
        square = square + part * part
    factor = lax.rsqrt(jnp.sum(square, axis=1, keepdims=True) / breadth + EPSILON)
    normed = []
    for head in range(HEADS):
        part = residual[:, head * HEAD_DIM : (head + 1) * HEAD_DIM] * factor
        normed.append((part * gain[head : head + 1, :].astype(jnp.float32)).astype(jnp.bfloat16))
    return normed


def layer_kernel(
    lengths_ref, source_ref, gate_scale_ref, up_scale_ref, down_scale_ref, key_hbm, queries_hbm, new_key_hbm, value_hbm,
    new_value_hbm, hidden_hbm, gain_hbm, ids_hbm, gates_hbm, talk_ids_hbm, talk_gates_hbm, gate_hbm, up_hbm, down_hbm,
    talker_gain_hbm, talk_gate_hbm, talk_up_hbm, talk_down_hbm,
    thinker_ref, talker_ref,
    keys, queries, new_key, values, new_value, hidden, gain, ids, gates, talk_ids, talk_gates, gate_w, up_w, down_w,
    talker_gain, talk_gate_w, talk_up_w, talk_down_w, load_sem, asked, scores, mixture, residual,
    rows_a, rows_b, kept, core_out, core_in, y_out, y_in, x_out, x_in, x_late_out, x_late_in, y_late_out, y_late_in,
    z_out, z_in, meta_out, meta_in, meta_rows, talk_rows, spaced, talk_out, talk_in, send_sem, recv_sem,
):
    f32, bf16 = jnp.float32, jnp.bfloat16
    wide, narrow = lax.axis_index("wide"), lax.axis_index("narrow")
    z, x, y, c = wide // 2, wide % 2, narrow // 2, narrow % 2
    half = 1024

    def peer(dz, bx, by, bc):
        there = (z + dz) % 4 if dz else z
        return (there * 2 + (1 - x if bx else x), (1 - y if by else y) * 2 + (1 - c if bc else c))

    loads = []
    for number, (source, target) in enumerate((
        (key_hbm, keys), (queries_hbm, queries), (new_key_hbm, new_key), (value_hbm, values),
        (new_value_hbm, new_value), (hidden_hbm, hidden), (gain_hbm, gain), (ids_hbm, ids), (gates_hbm, gates),
        (talk_ids_hbm, talk_ids), (talk_gates_hbm, talk_gates), (gate_hbm.at[0], gate_w), (up_hbm.at[0], up_w),
        (down_hbm.at[0], down_w), (talker_gain_hbm, talker_gain), (talk_gate_hbm.at[0], talk_gate_w),
        (talk_up_hbm.at[0], talk_up_w), (talk_down_hbm.at[0], talk_down_w),
    )):
        load = pltpu.make_async_copy(source, target, load_sem.at[number])
        load.start()
        loads.append(load)
    barrier = pltpu.get_barrier_semaphore()
    everyone = [
        (dz, bx, by, bc) for dz in range(4) for bx in range(2) for by in range(2) for bc in range(2) if dz or bx or by or bc
    ]
    for one in everyone:
        pl.semaphore_signal(barrier, inc=1, device_id=peer(*one), device_id_type=MESH)

    down_iota = lax.broadcasted_iota(jnp.int32, (16, 16), 0)
    along_iota = lax.broadcasted_iota(jnp.int32, (16, 16), 1)
    rel_down, rel_along, origin = (jnp.zeros((16, 16), jnp.int32) for _ in range(3))
    for position in range(16):
        number = source_ref[position]
        from_wide = lax.div(number, 64)
        from_z, from_x = lax.div(from_wide, 2), lax.rem(from_wide, 2)
        relative = lax.rem(from_z - z + 4, 4) * 2 + lax.rem(from_x + x, 2)
        rel_down = jnp.where(down_iota == position, relative, rel_down)
        rel_along = jnp.where(along_iota == position, relative, rel_along)
        origin = jnp.where(along_iota == position, lax.rem(number, 16), origin)
    same = rel_down == rel_along
    rank_down = jnp.sum(jnp.where(same & (along_iota < down_iota), 1.0, 0.0), axis=1, keepdims=True)
    rank_along = jnp.sum(jnp.where(same & (down_iota < along_iota), 1.0, 0.0), axis=0, keepdims=True)
    slot_down = rel_down.astype(f32) * 2 + rank_down
    slot_along = rel_along.astype(f32) * 2 + rank_along
    place = jnp.where(slot_down == along_iota.astype(f32), 1.0, 0.0).astype(bf16)
    place_across = jnp.where(slot_along == down_iota.astype(f32), 1.0, 0.0).astype(bf16)
    identity = jnp.where(down_iota == along_iota, 1.0, 0.0).astype(bf16)
    contract = (((1,), (1,)), ((), ()))
    lines = lax.broadcasted_iota(jnp.int32, (EXT, 16), 0)
    for number in range(7, 11):
        loads[number].wait()
    weight = jnp.zeros((EXT, 16), f32)
    for choice in range(TOP):
        weight = weight + jnp.where(ids[choice : choice + 1, :] == lines % 16, gates[choice : choice + 1, :], 0.0)
    high = weight.astype(bf16).astype(f32)
    split = jnp.where(lines < 16, high, weight - high).astype(bf16)
    extras = lax.dot_general(identity, split, contract, preferred_element_type=f32).astype(bf16)
    weight = jnp.zeros((EXT, 16), f32)
    for choice in range(TTOP):
        weight = weight + jnp.where(
            talk_ids[choice : choice + 1, :] == lines % 8, talk_gates[choice : choice + 1, :], 0.0
        )
    high = weight.astype(bf16).astype(f32)
    split = jnp.where(lines < 8, high, weight - high)
    split = jnp.where(lines == 4, origin[0:1, :].astype(f32), split).astype(bf16)
    by_slot = lax.dot_general(place_across, split, contract, preferred_element_type=f32)
    meta_out[...] = jnp.zeros_like(meta_out)
    for slot in range(8):
        meta_out[slot, 0:2, :] = by_slot[2 * slot : 2 * slot + 2, :]
    meta_in[0] = meta_out[0]

    for number in range(3):
        loads[number].wait()

    def before_values():
        for number in range(3, 7):
            loads[number].wait()

    normed = attention(
        hidden, queries, keys, values, new_key, new_value, lengths_ref, gain, asked, scores, mixture, residual,
        before_values,
    )
    for head in range(8):
        columns = slice(head * HEAD_DIM, (head + 1) * HEAD_DIM)
        rows_a[0, 0, :, columns] = normed[head]
        rows_b[0, 0, :, columns] = normed[8 + head]
    rows_a[0, 0, :, half:] = extras
    pl.semaphore_wait(barrier, len(everyone))

    pending = []

    def send(source, target, to):
        number = len(pending)
        copy = pltpu.make_async_remote_copy(
            src_ref=source, dst_ref=target, send_sem=send_sem.at[number], recv_sem=recv_sem.at[number],
            device_id=peer(*to), device_id_type=MESH,
        )
        copy.start()
        pending.append(copy)
        return copy

    to_x, to_y, to_c = (0, 1, 0, 0), (0, 0, 1, 0), (0, 0, 0, 1)
    a_x = [send(rows_a.at[0, 0], rows_a.at[2, 0], to_x)]
    b_y = [send(rows_b.at[0, 0], rows_b.at[4, 0], to_y)]
    a_z, b_z = {}, {}
    for step in (2, 1, 3):
        a_z[step] = send(rows_a.at[0, 0], rows_a.at[0, 4 - step], (step, 0, 0, 0))
        b_z[step] = send(rows_b.at[0, 0], rows_b.at[0, 4 - step], (step, 0, 0, 0))
    a_y = [send(rows_a.at[0, 0], rows_a.at[4, 0], to_y)]
    b_x = [send(rows_b.at[0, 0], rows_b.at[2, 0], to_x)]
    meta_copies = []
    for dz in range(4):
        for bx in range(2):
            if dz or bx:
                meta_copies.append(
                    send(meta_out.at[dz * 2 + bx], meta_in.at[(4 - dz) % 4 * 2 + bx], (dz, bx, 0, 0))
                )

    def scaled(weights, scale, row_block, column_blocks):
        rows = pl.ds(pl.multiple_of(row_block * BLK, BLK), BLK)
        for column in range(column_blocks):
            columns = slice(column * BLK, (column + 1) * BLK)
            weights[rows, columns] = (weights[rows, columns].astype(f32) * scale(row_block, column)).astype(bf16)

    loads[11].wait()
    loads[12].wait()

    def scale_inner(first, last):
        def body(row_block, carry):
            scaled(gate_w, lambda i, j: gate_scale_ref[j, 0, i], row_block, 3)
            scaled(up_w, lambda i, j: up_scale_ref[j, 0, i], row_block, 3)
            return carry

        lax.fori_loop(first, last, body, 0)

    scale_inner(0, 4)
    for step in (1, 3, 2):
        rel = 4 - step
        a_z[step].wait_recv()
        a_x.append(send(rows_a.at[0, rel], rows_a.at[2, rel], to_x))
        b_z[step].wait_recv()
        b_y.append(send(rows_b.at[0, rel], rows_b.at[4, rel], to_y))
        a_y.append(send(rows_a.at[0, rel], rows_a.at[4, rel], to_y))
        b_x.append(send(rows_b.at[0, rel], rows_b.at[2, rel], to_x))
    across = [send(rows_a.at[0], rows_a.at[1], to_c), send(rows_b.at[0], rows_b.at[1], to_c)]
    a_far, b_far = [], []
    for number, rel in enumerate((0, 3, 1, 2)):
        a_x[number].wait_recv()
        a_far.append(send(rows_a.at[2, rel], rows_a.at[6, rel], to_y))
        b_y[number].wait_recv()
        b_far.append(send(rows_b.at[4, rel], rows_b.at[6, rel], to_x))
        if number < 3:
            scale_inner(4 + number * 4, 8 + number * 4)
    across += [send(rows_a.at[2], rows_a.at[3], to_c), send(rows_b.at[4], rows_b.at[5], to_c)]
    loads[13].wait()

    def scale_outer(row_block, carry):
        scaled(down_w, lambda i, j: down_scale_ref[i, 0, j], row_block, 16)
        return carry

    lax.fori_loop(0, 3, scale_outer, 0)
    def weight_column(extras, first, second):
        lanes = lax.broadcasted_iota(jnp.int32, extras.shape, 1)
        return jnp.sum(jnp.where((lanes == first) | (lanes == second), extras.astype(f32), 0.0), axis=1, keepdims=True)

    expert = wide * 2 + narrow // 2

    def hidden_units(first, count):
        base, count = 2 * first, 2 * count
        left = rows_a[base : base + count].reshape(count * 64, half + EXT)
        right = rows_b[base : base + count].reshape(count * 64, half)
        weight = weight_column(left[:, half:], expert, expert + 16)
        left = left[:, :half]
        gated = jnp.dot(left, gate_w[:half], preferred_element_type=f32)
        gated = gated + jnp.dot(right, gate_w[half:], preferred_element_type=f32)
        lifted = jnp.dot(left, up_w[:half], preferred_element_type=f32)
        lifted = lifted + jnp.dot(right, up_w[half:], preferred_element_type=f32)
        return (jax.nn.silu(gated) * lifted).astype(bf16), weight

    core_copies = {}

    def process(first, count):
        middle, weight = hidden_units(first, count)
        for column in range(4):
            columns = slice(column * 512, (column + 1) * 512)
            part = jnp.dot(middle, down_w[:, columns], preferred_element_type=f32) * weight
            for at in range(count):
                kept[first + at, :, columns] = part[at * 128 : at * 128 + 64]
                core_out[first + at, :, columns] = part[at * 128 + 64 : at * 128 + 128].astype(bf16)
        for group in range(first, first + count):
            core_copies[group] = send(core_out.at[group], core_in.at[group], to_c)

    across[0].wait_recv()
    across[1].wait_recv()
    process(0, 1)
    for copy in a_y + b_x:
        copy.wait_recv()
    across += [send(rows_a.at[4], rows_a.at[5], to_c), send(rows_b.at[2], rows_b.at[3], to_c)]
    for copy in across[2:]:
        copy.wait_recv()
    process(1, 2)
    for copy in a_far + b_far:
        copy.wait_recv()
    across_far = [send(rows_a.at[6], rows_a.at[7], to_c), send(rows_b.at[6], rows_b.at[7], to_c)]
    for group in range(3):
        core_copies[group].wait_recv()
        kept[group] = kept[group] + core_in[group].astype(f32)
    for rel in range(4):
        y_out[0, rel] = kept[2, rel * 16 : (rel + 1) * 16, :half].astype(bf16)
        x_out[0, rel] = kept[1, rel * 16 : (rel + 1) * 16, half:].astype(bf16)
    near = [send(y_out.at[0], y_in.at[0], to_y), send(x_out.at[0], x_in.at[0], to_x)]
    for copy in across_far:
        copy.wait_recv()
    process(3, 1)
    core_copies[3].wait_recv()
    order = (2, 1, 3, 0)
    first_y, first_x = {}, {}
    for rel in order:
        span = slice(rel * 16, (rel + 1) * 16)
        y_out[1, rel] = (kept[3, span, :half] + core_in[3, span, :half].astype(f32)).astype(bf16)
        x_out[1, rel] = (kept[3, span, half:] + core_in[3, span, half:].astype(f32)).astype(bf16)
        first_y[rel] = send(y_out.at[1, rel], y_in.at[1, rel], to_y)
        first_x[rel] = send(x_out.at[1, rel], x_in.at[1, rel], to_x)
    late_x, late_y = {}, {}
    for rel in order:
        span = slice(rel * 16, (rel + 1) * 16)
        first_y[rel].wait_recv()
        x_late_out[rel] = (kept[1, span, :half] + y_in[1, rel].astype(f32)).astype(bf16)
        late_x[rel] = send(x_late_out.at[rel], x_late_in.at[rel], to_x)
        first_x[rel].wait_recv()
        y_late_out[rel] = (kept[2, span, half:] + x_in[1, rel].astype(f32)).astype(bf16)
        late_y[rel] = send(y_late_out.at[rel], y_late_in.at[rel], to_y)
    for copy in near:
        copy.wait_recv()
    z_copies = {}
    for rel in order:
        span = slice(rel * 16, (rel + 1) * 16)
        late_x[rel].wait_recv()
        late_y[rel].wait_recv()
        left = kept[0, span, :half] + y_in[0, rel].astype(f32) + x_late_in[rel].astype(f32)
        right = kept[0, span, half:] + x_in[0, rel].astype(f32) + y_late_in[rel].astype(f32)
        if rel:
            z_out[rel, :, :half] = left.astype(bf16)
            z_out[rel, :, half:] = right.astype(bf16)
            z_copies[rel] = send(z_out.at[rel], z_in.at[4 - rel], (rel, 0, 0, 0))
    sums = [left[:, :512], left[:, 512:], right[:, :512], right[:, 512:]]
    for rel in (1, 2, 3):
        z_copies[rel].wait_recv()
    for copy in meta_copies:
        copy.wait_recv()
    for load in loads[14:]:
        load.wait()
    square = jnp.zeros((16, 512), f32)
    finals = []
    for column in range(4):
        span = slice(column * 512, (column + 1) * 512)
        total = residual[:, span] + sums[column]
        for rel in (1, 2, 3):
            total = total + z_in[rel, :, span].astype(f32)
        final = total.astype(bf16)
        thinker_ref[:, span] = final
        final = final.astype(f32)
        finals.append(final)
        square = square + final * final
    factor = lax.rsqrt(jnp.sum(square, axis=1, keepdims=True) / 2048 + EPSILON)
    for slot in range(8):
        meta_rows[2 * slot : 2 * slot + 2, :] = meta_in[slot, 0:2, :]
    meta = meta_rows[...]
    picks = (meta[:, 4:5].astype(jnp.int32) == lax.broadcasted_iota(jnp.int32, (16, 16), 1)).astype(f32).astype(bf16)
    for column in range(4):
        span = slice(column * 512, (column + 1) * 512)
        for block in range(4):
            row = column * 4 + block
            normed = finals[column][:, block * BLK : (block + 1) * BLK] * factor
            normed = (normed * talker_gain[row : row + 1, :].astype(f32)).astype(bf16)
            talk_rows[0, :, row * BLK : (row + 1) * BLK] = jnp.dot(picks, normed, preferred_element_type=f32).astype(bf16)
    talk_rows[0, :, 2048:] = meta.astype(bf16)
    gathers = [send(talk_rows.at[0], talk_rows.at[v], (0, 0, v // 2, v % 2)) for v in (3, 2, 1)]
    for copy in gathers:
        copy.wait_recv()
    inputs = talk_rows[...].reshape(64, 2048 + EXT)
    weight = weight_column(inputs[:, 2048:], narrow, narrow + 8)
    inputs = inputs[:, :2048]
    gated = jnp.dot(inputs, talk_gate_w[...], preferred_element_type=f32)
    lifted = jnp.dot(inputs, talk_up_w[...], preferred_element_type=f32)
    middle = (jax.nn.silu(gated) * lifted).astype(bf16)
    result = jnp.dot(middle, talk_down_w[...], preferred_element_type=f32) * weight
    for column in range(8):
        spaced[:, column, :] = result[:, column * 128 : (column + 1) * 128]
    talk_out[...] = spaced[...].reshape(512, 128).astype(bf16).reshape(4, 8, 16, 128)
    backs = []
    for dz in (2, 1, 3, 0):
        for bx in range(2):
            for v in range(4):
                if dz or bx or v:
                    backs.append(
                        send(
                            talk_out.at[v, dz * 2 + bx], talk_in.at[v, (4 - dz) % 4 * 2 + bx], (dz, bx, v // 2, v % 2)
                        )
                    )
    talk_in[0, 0] = talk_out[0, 0]
    for copy in backs:
        copy.wait_recv()
    total = talk_in[0].astype(f32)
    for v in range(1, 4):
        total = total + talk_in[v].astype(f32)
    spaced[:16] = total.reshape(16, 8, 128)
    for column in range(8):
        part = spaced[:16, column, :].astype(bf16)
        talker_ref[:, column * 128 : (column + 1) * 128] = jnp.dot(
            place, part, preferred_element_type=f32
        ).astype(bf16)
    for copy in pending:
        copy.wait_send()


def local_fused(
    hidden_in, queries, cache_key, cache_value, new_key, new_value, lengths, norm_gain, gate_codes, gate_scale,
    up_codes, up_scale, down_codes, down_scale, think_ids, think_gates, talker_source, talker_gain, talk_gate_w,
    talk_up_w, talk_down_w, talk_ids, talk_gates,
):
    f32, bf16 = jnp.float32, jnp.bfloat16
    vmem, smem, hbm = (pl.BlockSpec(memory_space=s) for s in (pltpu.VMEM, pltpu.SMEM, pltpu.HBM))
    operands = [
        lengths, talker_source, jnp.transpose(gate_scale, (2, 0, 1)), jnp.transpose(up_scale, (2, 0, 1)),
        jnp.transpose(down_scale, (1, 0, 2)), cache_key, queries, new_key, cache_value, new_value, hidden_in,
        norm_gain.reshape(16, 128), think_ids.T, think_gates.T, talk_ids.T, talk_gates.T, gate_codes, up_codes,
        down_codes, talker_gain.reshape(16, 128), talk_gate_w, talk_up_w, talk_down_w,
    ]
    landing = []
    for operand in operands[5:]:
        shape = operand.shape[1:] if operand.shape[0] == 1 else operand.shape
        landing.append(pltpu.VMEM(shape, operand.dtype))
    rows, breadth = hidden_in.shape
    return pl.pallas_call(
        layer_kernel,
        out_shape=(jax.ShapeDtypeStruct((rows, breadth), bf16), jax.ShapeDtypeStruct((rows, 1024), bf16)),
        in_specs=[smem] * 5 + [hbm] * 18,
        out_specs=(vmem, vmem),
        scratch_shapes=landing
        + [
            pltpu.SemaphoreType.DMA((18,)),
            pltpu.VMEM((rows, HEADS, HEAD_DIM), f32),
            pltpu.VMEM((rows, HEADS, HEAD_DIM), f32),
            pltpu.VMEM((rows, HEADS, HEAD_DIM), f32),
            pltpu.VMEM((rows, breadth), f32),
            pltpu.VMEM((8, 4, 16, 1024 + EXT), bf16),
            pltpu.VMEM((8, 4, 16, 1024), bf16),
            pltpu.VMEM((4, 64, 2048), f32),
            pltpu.VMEM((4, 64, 2048), bf16),
            pltpu.VMEM((4, 64, 2048), bf16),
            pltpu.VMEM((2, 4, 16, 1024), bf16),
            pltpu.VMEM((2, 4, 16, 1024), bf16),
            pltpu.VMEM((2, 4, 16, 1024), bf16),
            pltpu.VMEM((2, 4, 16, 1024), bf16),
            pltpu.VMEM((4, 16, 1024), bf16),
            pltpu.VMEM((4, 16, 1024), bf16),
            pltpu.VMEM((4, 16, 1024), bf16),
            pltpu.VMEM((4, 16, 1024), bf16),
            pltpu.VMEM((4, 16, 2048), bf16),
            pltpu.VMEM((4, 16, 2048), bf16),
            pltpu.VMEM((8, 8, EXT), f32),
            pltpu.VMEM((8, 8, EXT), f32),
            pltpu.VMEM((16, EXT), f32),
            pltpu.VMEM((4, 16, 2048 + EXT), bf16),
            pltpu.VMEM((64, 8, 128), f32),
            pltpu.VMEM((4, 8, 16, 128), bf16),
            pltpu.VMEM((4, 8, 16, 128), bf16),
            pltpu.SemaphoreType.DMA((112,)),
            pltpu.SemaphoreType.DMA((112,)),
        ],
        compiler_params=pltpu.CompilerParams(
            collective_id=0, has_side_effects=True, vmem_limit_bytes=60 * 2**20
        ),
    )(*operands)


def solution(mesh):
    return jax.shard_map(
        local_fused if mesh.shape["wide"] == 8 and mesh.shape["narrow"] == 4 else local,
        mesh=mesh,
        in_specs=(
            P(("wide", "narrow"), None),
            P(("wide", "narrow"), None),
            P(("wide", "narrow"), None, None),
            P(("wide", "narrow"), None, None),
            P(("wide", "narrow"), None),
            P(("wide", "narrow"), None),
            P(("wide", "narrow")),
            P(),
            P(("wide", "narrow"), None, None),
            P(("wide", "narrow"), None, None),
            P(("wide", "narrow"), None, None),
            P(("wide", "narrow"), None, None),
            P(("wide", "narrow"), None, None),
            P(("wide", "narrow"), None, None),
            P(("wide", "narrow"), None),
            P(("wide", "narrow"), None),
            P(("wide", "narrow")),
            P(),
            P("narrow", None, None),
            P("narrow", None, None),
            P("narrow", None, None),
            P(("wide", "narrow"), None),
            P(("wide", "narrow"), None),
        ),
        out_specs=(P(("wide", "narrow"), None), P(("wide", "narrow"), None)),
        check_vma=False,
    )
```
